32 devices in a mesh: ckpt: 8 (over z, core), rows: 4 (over y, x).
Axes of the slice: x: 2, y: 2, z: 4, core: 2. Of those that a mesh axis runs over, the one named last changes fastest.
Arguments:
- deltas: bfloat16 [8, 4096, 14336], P('ckpt', 'rows'), may hold values from -24 to 24
- start_basis: bfloat16 [8, 14336, 64], P('ckpt', 'rows'), may hold values from -6 to 6
- edit_order: int32 [8], replicated, may hold values from 0 to 7, each once
Outputs:
- merged: bfloat16 [4096, 14336], P('rows', 'ckpt')
The draws below stay inside these ranges and needn't reach their ends.
Inputs may be any that keep to these rules, and one draw needn't show every extreme that they name: `edit_order`: a permutation: each of 0 to 7 appears once.
All inputs are finite; a program needn't handle non-finite values.
Results may differ from the reference program's by a relative error of at most 0.034.
Values may be sent and summed in bfloat16 or wider, within the bound.
No kernel may reach another device: no remote copies, remote signals or barrier semaphores. Data moves between devices by JAX's collectives and lax.ppermute only.
A program may use at most 128 MiB of HBM per device.

```python
import math
import jax
import jax.numpy as jnp
from jax import lax

D = 4096
FF = 14336
RANK = 64
SUB_ITERS = 2
NS_ITERS = 4
CKPT = 8
N_ROWS = 4


def unit_field(key, shape):
    return jax.random.normal(key, shape, jnp.float32)


def draw_deltas(key, part):
    common = unit_field(jax.random.fold_in(key, 11), (D, FF))
    pairing = jax.random.permutation(jax.random.fold_in(key, 12), N_ROWS)
    row_block = jnp.arange(D) // (D // N_ROWS)
    col_block = jnp.arange(FF) // (FF // N_ROWS)
    spike_factor = jnp.where(pairing[row_block][:, None] == col_block[None, :], 2.0, 1.0).astype(jnp.float32)
    factor = 2.0 * spike_factor

    def draw_single(ckpt_index):
        private = unit_field(jax.random.fold_in(key, 100 + ckpt_index), (D, FF))
        combined = factor * (math.sqrt(0.9) * common + math.sqrt(0.1) * private)
        return jnp.clip(combined, -24.0, 24.0).astype(jnp.bfloat16)
    return lax.map(draw_single, jnp.arange(CKPT))


def draw_start_basis(key, part):
    common = unit_field(jax.random.fold_in(key, 21), (FF, RANK))
    private = unit_field(jax.random.fold_in(key, 22), (CKPT, FF, RANK))
    combined = math.sqrt(0.9) * common[None, :, :] + math.sqrt(0.1) * private
    return jnp.clip(combined, -6.0, 6.0).astype(jnp.bfloat16)


def setup_inputs(seed: int = 0) -> dict:
    key_of = jax.random.split(jax.random.key(seed), 4)
    return {
        "deltas": draw_deltas(jax.random.fold_in(key_of[3], 71), 0),
        "start_basis": draw_start_basis(jax.random.fold_in(key_of[3], 71), 0),
        "edit_order": jax.random.permutation(key_of[2], CKPT).astype(jnp.int32),
    }


def orthonormal(raw):
    gram_matrix = jnp.dot(raw.T, raw, precision=lax.Precision.HIGHEST)
    lower_factor = jnp.linalg.cholesky(gram_matrix)
    basis_new = lax.linalg.triangular_solve(lower_factor, raw, left_side=False, lower=True, transpose_a=True)
    return (basis_new.astype(jnp.bfloat16), lower_factor)

def subspace(pair):
    changes, start = pair
    basis_now = start
    left_basis = jnp.zeros((D, RANK), jnp.bfloat16)
    lower_factor = jnp.zeros((RANK, RANK), jnp.float32)
    for sweep in range(SUB_ITERS):
        left_raw = jnp.dot(changes.astype(jnp.float32), basis_now.astype(jnp.float32), preferred_element_type=jnp.float32)
        left_basis, unused = orthonormal(left_raw)
        right_raw = lax.dot_general(changes.astype(jnp.float32), left_basis.astype(jnp.float32), (((0,), (0,)), ((), ())), preferred_element_type=jnp.float32)
        basis_now, lower_factor = orthonormal(right_raw)
    return (left_basis, basis_now, lower_factor)

def whiten(stacked):
    current = stacked
    for step in range(NS_ITERS):
        gram_matrix = jnp.dot(current.T.astype(jnp.float32), current.astype(jnp.float32), preferred_element_type=jnp.float32)
        if step == 0:
            lead_factor = 1.5 / math.sqrt(CKPT)
            tail_factor = -0.5 / (CKPT * math.sqrt(CKPT))
        else:
            lead_factor = 1.5
            tail_factor = -0.5
        product = jnp.dot(current.astype(jnp.float32), gram_matrix, precision=lax.Precision.HIGHEST)
        current = (lead_factor * current.astype(jnp.float32) + tail_factor * product).astype(jnp.bfloat16)
    return current

def reference(deltas, start_basis, edit_order):
    lefts, rights, lowers = lax.map(subspace, (deltas, start_basis))
    left_stack = lefts.transpose(1, 0, 2).reshape(D, CKPT * RANK)
    right_stack = rights.transpose(1, 0, 2).reshape(FF, CKPT * RANK)
    left_white = whiten(left_stack)
    right_white = whiten(right_stack)
    weights = (1 + edit_order).astype(jnp.float32) / CKPT
    middles = lowers * weights[:, None, None]
    left_blocks = left_white.reshape(D, CKPT, RANK).astype(jnp.float32)
    scaled_left = jnp.einsum('dcr,crs->dcs', left_blocks, middles, precision=lax.Precision.HIGHEST)
    scaled_left = scaled_left.astype(jnp.bfloat16).reshape(D, CKPT * RANK)
    merged = lax.dot_general(scaled_left.astype(jnp.float32), right_white.astype(jnp.float32), (((1,), (1,)), ((), ())), preferred_element_type=jnp.float32)
    return merged.astype(jnp.bfloat16)
```

```python
import functools
import math

import jax
import jax.numpy as jnp
from jax import lax
from jax.experimental import pallas as pl
from jax.experimental.pallas import tpu as pltpu
from jax.sharding import PartitionSpec as P

NS_ITERS = 4
LIFT = 2.0**40
VMEM_BYTES = 56 * 1024 * 1024
HIGH = lax.Precision.HIGHEST


def sweep_kernel(pieces, lift, delta_ref, basis_ref, left_ref, right_ref, total):
    step = pl.program_id(0)
    width = basis_ref.shape[2]
    part = None
    for piece in range(basis_ref.shape[0]):
        term = lax.dot_general(
            delta_ref[:, piece * width:(piece + 1) * width],
            basis_ref[piece],
            (((1,), (1,)), ((), ())),
            preferred_element_type=jnp.float32,
        )
        part = term if part is None else part + term
    left = (jnp.transpose(part) * lift).astype(jnp.bfloat16)
    left_ref[...] = left

    @pl.when(step == 0)
    def _():
        total[...] = jnp.zeros_like(total)

    chunk = pieces[0][1]
    for start, size, _ in pieces:
        total[:, start:start + size] += lax.dot_general(
            left,
            delta_ref[:, start:start + size],
            (((1,), (0,)), ((), ())),
            preferred_element_type=jnp.float32,
        )

    @pl.when(step == pl.num_programs(0) - 1)
    def _():
        for start, size, (group, offset) in pieces:
            right_ref[group, :, offset:offset + size] = total[:, start:start + size].astype(jnp.bfloat16)


def sweep(changes, basis, lift, groups, padded):
    rows, cols = changes.shape
    rank = basis.shape[1]
    real = cols // groups
    block = min(256, rows)
    pieces = []
    for group in range(groups):
        offset = 0
        while offset < real:
            size = min(1792, real - offset)
            pieces.append((group * real + offset, size, (group, offset)))
            offset += size
    return pl.pallas_call(
        functools.partial(sweep_kernel, tuple(pieces), lift),
        grid=(rows // block,),
        in_specs=[
            pl.BlockSpec((block, cols), lambda i: (i, 0)),
            pl.BlockSpec(basis.shape, lambda i: (0, 0, 0)),
        ],
        out_specs=[
            pl.BlockSpec((rank, block), lambda i: (0, i)),
            pl.BlockSpec((groups, rank, padded), lambda i: (0, 0, 0)),
        ],
        out_shape=[
            jax.ShapeDtypeStruct((rank, rows), jnp.bfloat16),
            jax.ShapeDtypeStruct((groups, rank, padded), jnp.bfloat16),
        ],
        scratch_shapes=[pltpu.VMEM((rank, cols), jnp.float32)],
        compiler_params=pltpu.CompilerParams(vmem_limit_bytes=VMEM_BYTES),
        name="sweep",
    )(changes, basis)


def spread(own, axis):
    count = lax.axis_size(axis)
    index = lax.axis_index(axis)
    parts = [own]
    for gap in range(1, count):
        parts.append(lax.ppermute(own, axis, [(src, src ^ gap) for src in range(count)]))
    stacked = jnp.stack(parts)
    order = jnp.arange(count) ^ index
    return jnp.take(stacked, order, axis=0)


def collect(parts, axis):
    count = lax.axis_size(axis)
    index = lax.axis_index(axis)
    total = lax.dynamic_index_in_dim(parts, index, keepdims=False).astype(jnp.float32)
    for gap in range(1, count):
        leaving = lax.dynamic_index_in_dim(parts, index ^ gap, keepdims=False)
        total += lax.ppermute(leaving, axis, [(src, src ^ gap) for src in range(count)]).astype(jnp.float32)
    return total


def inverse_factor(grams):
    lower = jnp.linalg.cholesky(grams)
    unit = jnp.broadcast_to(jnp.eye(grams.shape[-1], dtype=jnp.float32), grams.shape)
    return lax.linalg.triangular_solve(lower, unit, left_side=False, lower=True, transpose_a=True)


def block_diagonal(blocks):
    count, rank, _ = blocks.shape
    unit = jnp.eye(count, dtype=blocks.dtype)
    return (unit[:, None, :, None] * blocks[:, :, None, :]).reshape(count * rank, count * rank)


def own_blocks(gram, count, rank):
    return jnp.stack([gram[c * rank:(c + 1) * rank, c * rank:(c + 1) * rank] for c in range(count)])


def mul(a, b):
    return jnp.dot(a, b, precision=HIGH)


def halves(x):
    high = x.astype(jnp.bfloat16)
    return high, (x - high.astype(jnp.float32)).astype(jnp.bfloat16)


def whiten_kernel(count, gram_ref, diag_ref, out_ref, gram, factor, spare, high, low):
    size = gram_ref.shape[0]
    strip = min(256, size)

    def product(a_ref, b_ref, c_ref, transposed=False, lead=0.0, tail=1.0):
        high[...], low[...] = halves(b_ref[...])
        contract = (((0 if transposed else 1,), (0,)), ((), ()))

        def one(index, _):
            rows = pl.ds(pl.multiple_of(index * strip, strip), strip)
            a = a_ref[:, rows] if transposed else a_ref[rows, :]
            a_high, a_low = halves(a)
            dot = functools.partial(lax.dot_general, dimension_numbers=contract, preferred_element_type=jnp.float32)
            c = tail * (dot(a_high, high[...]) + dot(a_high, low[...]) + dot(a_low, high[...]))
            if not transposed and lead:
                c = c + lead * a
            c_ref[rows, :] = c
            return 0

        lax.fori_loop(0, size // strip, one, 0)

    product(gram_ref, diag_ref, spare)
    product(diag_ref, spare, gram, transposed=True)
    unit = (
        lax.broadcasted_iota(jnp.int32, (size, size), 0) == lax.broadcasted_iota(jnp.int32, (size, size), 1)
    ).astype(jnp.float32)
    lead, tail = 1.5 / math.sqrt(count), -0.5 / (count * math.sqrt(count))
    out_ref[...] = lead * unit + tail * gram[...]

    def one_step(step, _):
        first = step == 1
        lead = jnp.where(first, 1.5 / math.sqrt(count), 1.5)
        tail = jnp.where(first, -0.5 / (count * math.sqrt(count)), -0.5)
        factor[...] = gram[...]
        product_dyn(gram, factor, spare, lead, tail)
        product_dyn(spare, factor, gram, lead, tail)
        factor[...] = gram[...]
        product_dyn(out_ref, factor, spare, 1.5, -0.5)
        out_ref[...] = spare[...]
        return 0

    def product_dyn(a_ref, b_ref, c_ref, lead, tail):
        high[...], low[...] = halves(b_ref[...])

        def one(index, _):
            rows = pl.ds(pl.multiple_of(index * strip, strip), strip)
            a = a_ref[rows, :]
            a_high, a_low = halves(a)
            dot = functools.partial(jnp.dot, preferred_element_type=jnp.float32)
            c = dot(a_high, high[...]) + dot(a_high, low[...]) + dot(a_low, high[...])
            c_ref[rows, :] = lead * a + tail * c
            return 0

        lax.fori_loop(0, size // strip, one, 0)

    lax.fori_loop(1, NS_ITERS, one_step, 0)


def whitener(gram, diag, count):
    size = gram.shape[0]
    return pl.pallas_call(
        functools.partial(whiten_kernel, count),
        out_shape=jax.ShapeDtypeStruct((size, size), jnp.float32),
        scratch_shapes=[pltpu.VMEM((size, size), jnp.float32)] * 3 + [pltpu.VMEM((size, size), jnp.bfloat16)] * 2,
        compiler_params=pltpu.CompilerParams(vmem_limit_bytes=VMEM_BYTES),
        name="whiten",
    )(gram, diag)


def body(deltas, start_basis, edit_order):
    changes = deltas[0]
    start = jnp.transpose(start_basis[0])
    rank = start.shape[0]
    rows_count = lax.axis_size("rows")
    ckpt_count = lax.axis_size("ckpt")
    ckpt_index = lax.axis_index("ckpt")
    cols = changes.shape[1]

    basis = lax.all_gather(start, "rows", axis=0)
    _, right = sweep(changes, basis, LIFT, rows_count, cols // rows_count)
    right = collect(right, "rows").astype(jnp.bfloat16)
    right_all = spread(right, "rows")
    peak = jnp.max(jnp.abs(right_all)).astype(jnp.float32)
    scaled = right_all.astype(jnp.float32) * (1.0 / peak)
    gram = jnp.einsum("nrf,nsf->rs", scaled, scaled, precision=HIGH)
    triangle = inverse_factor(gram[None])[0]
    basis = jnp.einsum("rs,nrf->nsf", triangle, scaled, precision=HIGH).astype(jnp.bfloat16)

    block = cols // ckpt_count
    padded = -(-block // (rows_count * 128)) * 128
    left, right = sweep(changes, basis, 1.0, ckpt_count, padded * rows_count)
    inside = jnp.arange(padded * rows_count) < block
    right = jnp.where(inside, right, 0)
    right = right.reshape(ckpt_count, rank, rows_count, padded).transpose(2, 0, 1, 3)
    right = collect(right, "rows").astype(jnp.bfloat16)
    left_all = lax.all_gather(left, "ckpt", axis=0, tiled=True)
    right = lax.all_to_all(right, "ckpt", split_axis=0, concat_axis=0, tiled=True)
    right = right.reshape(ckpt_count * rank, padded)
    right_all = lax.all_gather(right, "rows", axis=0)

    nt = (((1,), (1,)), ((), ()))
    gram_left = lax.psum(
        lax.dot_general(left_all, left_all, nt, preferred_element_type=jnp.float32), "rows"
    )
    left_t = inverse_factor(own_blocks(gram_left, ckpt_count, rank))
    left_diag = block_diagonal(left_t)
    left_p = whitener(gram_left, left_diag, ckpt_count)

    gram_right = lax.psum(
        lax.dot_general(right, right, nt, preferred_element_type=jnp.float32), ("ckpt", "rows")
    )
    right_own = own_blocks(gram_right, ckpt_count, rank)
    right_t = inverse_factor(right_own)
    right_diag = block_diagonal(right_t)
    right_p = whitener(gram_right, right_diag, ckpt_count)

    weight = (1 + edit_order).astype(jnp.float32) / ckpt_count
    middle = jnp.einsum("crs,crt,ctu->csu", left_t, right_own, right_t, precision=HIGH)
    middle = block_diagonal(middle * weight[:, None, None])
    left_mix = mul(mul(left_diag, left_p), middle)
    right_mix = mul(right_p, right_diag.T)
    mixed = jnp.dot(left_all.T, mul(left_mix, right_mix).astype(jnp.bfloat16), preferred_element_type=jnp.float32)
    merged = jnp.einsum(
        "dk,nkf->dnf", mixed.astype(jnp.bfloat16), right_all, preferred_element_type=jnp.float32
    )
    merged = merged.reshape(merged.shape[0], -1)[:, :block]
    return merged.astype(jnp.bfloat16)


def solution(mesh):
    return jax.shard_map(
        body,
        mesh=mesh,
        in_specs=(P("ckpt", "rows", None), P("ckpt", "rows", None), P()),
        out_specs=P("rows", "ckpt"),
        check_vma=False,
    )
```

```python
import functools
import math

import jax
import jax.numpy as jnp
from jax import lax
from jax.experimental import pallas as pl
from jax.experimental.pallas import tpu as pltpu
from jax.sharding import PartitionSpec as P

NS_ITERS = 4
LIFT = 2.0**60
VMEM_BYTES = 56 * 1024 * 1024
F32 = jnp.float32
BF16 = jnp.bfloat16
NN = (((1,), (0,)), ((), ()))
NT = (((1,), (1,)), ((), ()))
TN = (((0,), (0,)), ((), ()))


def dot(a, b, dims=NN):
    return lax.dot_general(a, b, dims, preferred_element_type=F32)


def halves(x):
    high = x.astype(BF16)
    return high, (x - high.astype(F32)).astype(BF16)


def dot_wide(a, b, dims=NN):
    a_high, a_low = halves(a)
    b_high, b_low = halves(b)
    return dot(a_high, b_high, dims) + (dot(a_high, b_low, dims) + dot(a_low, b_high, dims))


def power_scale(peak, root=False):
    scale = jnp.ones_like(peak)
    full = jnp.ones_like(peak)
    for exponent in (64, 32, 16, 8, 4, 2, 1):
        big = peak * full >= 2.0**exponent
        full = jnp.where(big, full * 2.0**-exponent, full)
        scale = jnp.where(big, scale * 2.0 ** -(exponent // 2), scale)
    for exponent in (64, 32, 16, 8, 4, 2, 1):
        small = peak * full * 2.0**exponent < 2.0
        full = jnp.where(small, full * 2.0**exponent, full)
        scale = jnp.where(small, scale * 2.0 ** (exponent // 2), scale)
    return scale if root else full


def inverse_factor(gram, work):
    rank = gram.shape[0]
    index = lax.broadcasted_iota(jnp.int32, (rank, 1), 0)
    lane = lax.broadcasted_iota(jnp.int32, (rank, 2 * rank), 1)
    work[:, :rank] = (lax.broadcasted_iota(jnp.int32, (rank, rank), 1) == index).astype(F32)
    work[:, rank:] = gram
    table = work[...]
    for k in range(rank - 1):
        row = table[k:k + 1, :]
        inverse = 1.0 / row[:, rank + k:rank + k + 1]
        column = table[:, rank + k:rank + k + 1]
        table = table - jnp.where(index > k, column * inverse, 0.0) * row
    pivots = jnp.sum(jnp.where(lane == index + rank, table, 0.0), axis=1, keepdims=True)
    work[...] = table * lax.rsqrt(pivots)
    return work[:, :rank]


def load_delta(delta_hbm, delta, sems):
    chunks = sems.shape[0]
    size = delta.shape[0] // chunks
    copies = []
    for chunk in range(chunks):
        rows = pl.ds(chunk * size, size)
        copies.append(pltpu.make_async_copy(delta_hbm.at[rows, :], delta.at[rows, :], sems.at[chunk]))
    for copy in copies:
        copy.start()
    return copies


def left_product(copies, delta, basis, store):
    rows, cols = delta.shape
    per = rows // len(copies)
    block = min(256, rows)
    width = 3584 if cols % 3584 == 0 else cols
    for start in range(0, rows, block):
        for chunk in range(start // per, (start + block) // per):
            copies[chunk].wait()
        part = None
        for at in range(0, cols, width):
            term = dot(basis[:, at:at + width], delta[start:start + block, at:at + width], NT)
            part = term if part is None else part + term
        store(start, block, part)


def first_kernel(count, place_ref, delta_hbm, *refs):
    pieces, rights = refs[:count], refs[count:2 * count]
    delta, basis, left, sems = refs[2 * count:]
    copies = load_delta(delta_hbm, delta, sems)
    width = pieces[0].shape[1]
    place = place_ref[0]
    peak = None
    for piece in pieces:
        most = jnp.max(jnp.abs(piece[...].astype(F32)), keepdims=True)
        peak = most if peak is None else jnp.maximum(peak, most)
    scale = power_scale(peak)
    for gap, piece in enumerate(pieces):
        at = pl.multiple_of((place ^ gap) * width, 128)
        basis[:, pl.ds(at, width)] = (piece[...].astype(F32) * scale).astype(BF16)

    def store(start, block, part):
        left[:, start:start + block] = (part * LIFT).astype(BF16)

    left_product(copies, delta, basis, store)
    for gap, right in enumerate(rights):
        at = pl.multiple_of((place ^ gap) * width, 128)
        right[...] = dot(left[...], delta[:, pl.ds(at, width)]).astype(BF16)


def second_kernel(count, groups, place_ref, delta_hbm, *refs):
    pieces, left, gram, rights = refs[:count], refs[count], refs[count + 1], refs[count + 2:2 * count + 2]
    delta, basis, work, sems = refs[2 * count + 2:]
    copies = load_delta(delta_hbm, delta, sems)
    width = pieces[0].shape[1]
    rank = left.shape[0]
    place = place_ref[0]
    peak = None
    for piece in pieces:
        most = jnp.max(jnp.abs(piece[...].astype(F32)), keepdims=True)
        peak = most if peak is None else jnp.maximum(peak, most)
    scale = power_scale(peak)
    second = power_scale(peak * (1.0 / LIFT), root=True)
    right_gram = None
    for gap, piece in enumerate(pieces):
        at = pl.multiple_of((place ^ gap) * width, 128)
        scaled = (piece[...].astype(F32) * scale).astype(BF16)
        basis[:, pl.ds(at, width)] = scaled
        term = dot(scaled, scaled, NT)
        right_gram = term if right_gram is None else right_gram + term
    inverse = inverse_factor(right_gram, work) * second
    high, low = halves(inverse)
    step = 1792 if width % 1792 == 0 else width
    for at in range(0, count * width, step):
        old = basis[:, at:at + step]
        basis[:, at:at + step] = (dot(high, old) + dot(low, old)).astype(BF16)

    def store(start, block, part):
        left[:, start:start + block] = part.astype(BF16)

    left_product(copies, delta, basis, store)
    gram[...] = dot(left[...], left[...], NT)
    real = delta.shape[1] // groups
    padded = rights[0].shape[2]
    left_now = left[...]
    for gap, right in enumerate(rights):
        slot = place ^ gap
        for group in range(groups):
            for spot in range(count):
                size = max(0, min(padded, real - spot * padded))
                if size == padded and spot:
                    continue
                @pl.when(slot == spot if size < padded else slot * padded + padded <= real)
                def _(right=right, group=group, size=size):
                    if size < padded:
                        right[group] = jnp.zeros_like(right[group])
                    if size:
                        at = pl.multiple_of(group * real + slot * padded, 128)
                        right[group, :, :size] = dot(left_now, delta[:, pl.ds(at, size)]).astype(BF16)


def sweep_call(kernel, place, changes, pieces, out_shape, extra, name):
    rows, cols = changes.shape
    rank = pieces[0].shape[0]
    vmem = pl.BlockSpec(memory_space=pltpu.VMEM)
    chunks = max(1, rows // 128)
    return pl.pallas_call(
        kernel,
        in_specs=[pl.BlockSpec(memory_space=pltpu.SMEM), pl.BlockSpec(memory_space=pl.ANY)] + [vmem] * len(pieces),
        out_specs=[vmem] * len(out_shape),
        out_shape=out_shape,
        scratch_shapes=[pltpu.VMEM((rows, cols), BF16), pltpu.VMEM((rank, cols), BF16), extra,
                        pltpu.SemaphoreType.DMA((chunks,))],
        compiler_params=pltpu.CompilerParams(vmem_limit_bytes=VMEM_BYTES),
        name=name,
    )(place, changes, *pieces)


def small_call(kernel, out_shape, args, scratch=(), name=None, scalars=0):
    spec = lambda i: pl.BlockSpec(memory_space=pltpu.SMEM if i < scalars else pltpu.VMEM)
    return pl.pallas_call(
        kernel,
        in_specs=[spec(i) for i in range(len(args))],
        out_specs=[pl.BlockSpec(memory_space=pltpu.VMEM)] * len(out_shape),
        out_shape=out_shape,
        scratch_shapes=list(scratch),
        compiler_params=pltpu.CompilerParams(vmem_limit_bytes=VMEM_BYTES),
        name=name,
    )(*args)


def left_kernel(count, left, *refs):
    grams, (out, inverse, work) = refs[:count], refs[count:]
    total = grams[0][...]
    for gram in grams[1:]:
        total = total + gram[...]
    factor = inverse_factor(total, work)
    inverse[...] = factor
    high, low = halves(factor)
    out[...] = (dot(high, left[...]) + dot(low, left[...])).astype(BF16)


def right_sum_kernel(count, *refs):
    parts, (total, gram) = refs[:count], refs[count:]
    result = None
    for group in range(total.shape[0]):
        value = parts[0][group].astype(F32)
        for part in parts[1:]:
            value = value + part[group].astype(F32)
        total[group] = value
        term = dot_wide(value, value, NT)
        result = term if result is None else result + term
    gram[...] = result


def right_kernel(count, groups, place_ref, total, left_inverse, *refs):
    grams, outs, (middle, work) = refs[:count], refs[count:count + groups], refs[count + groups:]
    gram = grams[0][...]
    for other in grams[1:]:
        gram = gram + other[...]
    factor = inverse_factor(gram, work)
    middle[...] = dot_wide(left_inverse[...], dot_wide(gram, factor, NT))
    high, low = halves(factor)
    for gap, out in enumerate(outs):
        value_high, value_low = halves(total[place_ref[0] ^ gap])
        out[...] = (dot(high, value_high) + (dot(high, value_low) + dot(low, value_high))).astype(BF16)


def gram_kernel(groups, count, place_ref, *refs):
    pieces, stack, slabs = refs[:groups], refs[groups], refs[groups + 1:]
    rank = pieces[0].shape[0]
    for gap, piece in enumerate(pieces):
        at = pl.multiple_of((place_ref[0] ^ gap) * rank, rank)
        stack[pl.ds(at, rank), :] = piece[...]
    size = stack.shape[0] // count
    for gap, slab in enumerate(slabs):
        at = pl.multiple_of((place_ref[1] ^ gap) * size, size)
        slab[...] = dot(stack[pl.ds(at, size), :], stack[...], NT).astype(BF16)


def polish(count, gram, product, spare, side):
    size = gram.shape[0]
    strip = min(128, size)
    eye = (
        lax.broadcasted_iota(jnp.int32, (size, size), 0) == lax.broadcasted_iota(jnp.int32, (size, size), 1)
    ).astype(F32)
    lead, tail = 1.5 / math.sqrt(count), -0.5 / (count * math.sqrt(count))
    product[...] = lead * eye + tail * gram[...]

    def multiply(a_ref, c_ref, lead, tail):
        def one(index, _):
            rows = pl.ds(pl.multiple_of(index * strip, strip), strip)
            a = a_ref[rows, :]
            c_ref[rows, :] = lead * a + tail * dot(a.astype(BF16), side[...])
            return 0

        lax.fori_loop(0, size // strip, one, 0)

    def step(index, _):
        first = index == 1
        before = jnp.where(first, lead, 1.5)
        after = jnp.where(first, tail, -0.5)
        side[...] = gram[...].astype(BF16)
        multiply(gram, spare, before, after)
        multiply(spare, gram, before, after)
        side[...] = gram[...].astype(BF16)
        multiply(product, product, 1.5, -0.5)
        return 0

    lax.fori_loop(1, NS_ITERS, step, 0)


def left_mix_kernel(count, gram_ref, stack, middle, out, gram, product, spare, side):
    gram[...] = gram_ref[...].astype(F32)
    polish(count, gram, product, spare, side)
    rank = middle.shape[1]
    for index in range(count):
        rows = pl.ds(index * rank, rank)
        spare[rows, :] = dot_wide(jnp.transpose(middle[index]), product[rows, :])
    side[...] = spare[...].astype(BF16)
    out[...] = dot(side[...], stack[...]).astype(BF16)


def merge_kernel(count, ckpt_count, place_ref, mixed, *refs):
    slabs, pieces, out = refs[:count], refs[count:2 * count], refs[2 * count]
    gram, product, spare, side, wide = refs[2 * count + 1:]
    size = gram.shape[0]
    slab_rows = size // count

    @pl.when(pl.program_id(0) == 0)
    def _():
        for gap, slab in enumerate(slabs):
            at = pl.multiple_of((place_ref[0] ^ gap) * slab_rows, slab_rows)
            gram[pl.ds(at, slab_rows), :] = slab[...].astype(F32)
        padded = pieces[0].shape[1]
        for gap, piece in enumerate(pieces):
            at = pl.multiple_of((place_ref[0] ^ gap) * padded, 128)
            wide[:, pl.ds(at, padded)] = piece[...]
        polish(ckpt_count, gram, product, spare, side)
        side[...] = product[...].astype(BF16)

    turned = jnp.transpose(dot(side[...], mixed[...])).astype(BF16)
    real = out.shape[1]
    out[...] = dot(turned, wide[:, :real]).astype(BF16)


def permute(value, axis, gap):
    count = lax.axis_size(axis)
    return lax.ppermute(value, axis, [(source, source ^ gap) for source in range(count)])


def spread(value, axis):
    return [value] + [permute(value, axis, gap) for gap in range(1, lax.axis_size(axis))]


def swap(values, axis):
    return [values[0]] + [permute(value, axis, gap) for gap, value in enumerate(values) if gap]


def body(deltas, start_basis, edit_order):
    changes = deltas[0]
    start = jnp.transpose(start_basis[0])
    rank, width = start.shape
    rows, cols = changes.shape
    count = lax.axis_size("rows")
    groups = lax.axis_size("ckpt")
    row_place = lax.axis_index("rows").astype(jnp.int32)
    ckpt_place = lax.axis_index("ckpt").astype(jnp.int32)
    at_row = row_place[None]
    at_ckpt = ckpt_place[None]
    at_both = jnp.stack([ckpt_place, row_place])
    shape = jax.ShapeDtypeStruct
    square = shape((rank, rank), F32)
    work = pltpu.VMEM((rank, 2 * rank), F32)

    parts = sweep_call(
        functools.partial(first_kernel, count), at_row, changes, spread(start, "rows"),
        [shape((rank, width), BF16)] * count, pltpu.VMEM((rank, rows), BF16), "first_sweep",
    )
    arrived = swap(parts, "rows")
    right = sum(part.astype(F32) for part in arrived).astype(BF16)

    block = cols // groups
    padded = -(-block // (count * 128)) * 128
    left, left_gram, *parts = sweep_call(
        functools.partial(second_kernel, count, groups), at_row, changes, spread(right, "rows"),
        [shape((rank, rows), BF16), square] + [shape((groups, rank, padded), BF16)] * count, work, "second_sweep",
    )
    arrived = swap(parts, "rows")

    left_unit, left_inverse = small_call(
        functools.partial(left_kernel, count), [shape((rank, rows), BF16), square],
        [left] + spread(left_gram, "rows"), [work], "left_unit",
    )
    left_stack = lax.all_gather(left_unit, "ckpt", axis=0, tiled=True)
    left_gram = lax.psum(dot(left_stack, left_stack, NT).astype(BF16), "rows")

    total, right_gram = small_call(
        functools.partial(right_sum_kernel, count), [shape((groups, rank, padded), F32), square], arrived,
        name="right_sum",
    )
    *leaving, middle = small_call(
        functools.partial(right_kernel, count, groups), [shape((rank, padded), BF16)] * groups + [square],
        [at_ckpt, total, left_inverse] + spread(right_gram, "rows"), [work], "right_unit", scalars=1,
    )
    pieces = swap(leaving, "ckpt")
    weight = (1 + jnp.sum(jnp.where(jnp.arange(groups) == ckpt_place, edit_order, 0))).astype(F32) / groups
    middles = lax.all_gather(middle * weight, "ckpt", axis=0)

    size = groups * rank
    table = pltpu.VMEM((size, size), F32)
    tables = [table, table, table, pltpu.VMEM((size, size), BF16)]
    right_stack, *slabs = small_call(
        functools.partial(gram_kernel, groups, count),
        [shape((size, padded), BF16)] + [shape((size // count, size), BF16)] * count,
        [at_both] + pieces, name="right_gram", scalars=1,
    )
    slab = sum(part.astype(F32) for part in swap(slabs, "rows"))
    two = slab.reshape(2, size // count // 2, size).astype(BF16)
    half = lax.rem(ckpt_place, 2)
    mine = lax.dynamic_index_in_dim(two, half, keepdims=False).astype(F32)
    mine += permute(lax.dynamic_index_in_dim(two, 1 - half, keepdims=False), "ckpt", 1).astype(F32)
    mine = mine.astype(BF16)
    whole = mine.astype(F32)
    for gap in range(2, groups, 2):
        whole += permute(mine, "ckpt", gap).astype(F32)
    whole = whole.astype(BF16)
    other = permute(whole, "ckpt", 1)
    slab = jnp.concatenate([jnp.where(half == 0, whole, other), jnp.where(half == 0, other, whole)])
    slabs = spread(slab, "rows")
    right_all = spread(right_stack, "rows")

    (mixed,) = small_call(
        functools.partial(left_mix_kernel, groups), [shape((size, rows), BF16)], [left_gram, left_stack, middles],
        tables, "left_mix",
    )
    step = min(256, rows)
    full = lambda value: pl.BlockSpec(value.shape, lambda i: (0, 0))
    return pl.pallas_call(
        functools.partial(merge_kernel, count, groups),
        grid=(rows // step,),
        in_specs=[pl.BlockSpec(memory_space=pltpu.SMEM), pl.BlockSpec((size, step), lambda i: (0, i))]
        + [full(value) for value in slabs + right_all],
        out_specs=pl.BlockSpec((step, block), lambda i: (i, 0)),
        out_shape=shape((rows, block), BF16),
        scratch_shapes=tables + [pltpu.VMEM((size, padded * count), BF16)],
        compiler_params=pltpu.CompilerParams(vmem_limit_bytes=VMEM_BYTES),
        name="merge",
    )(at_row, mixed, *slabs, *right_all)


def solution(mesh):
    return jax.shard_map(
        body,
        mesh=mesh,
        in_specs=(P("ckpt", "rows", None), P("ckpt", "rows", None), P()),
        out_specs=P("rows", "ckpt"),
        check_vma=False,
    )
```

```python
import functools
import math

import jax
import jax.numpy as jnp
from jax import lax
from jax.experimental import pallas as pl
from jax.experimental.pallas import tpu as pltpu
from jax.sharding import PartitionSpec as P

NS_ITERS = 4
LIFT = 2.0**60
VMEM_BYTES = 56 * 1024 * 1024
F32 = jnp.float32
BF16 = jnp.bfloat16
NN = (((1,), (0,)), ((), ()))
NT = (((1,), (1,)), ((), ()))
TN = (((0,), (0,)), ((), ()))


def dot(a, b, dims=NN):
    return lax.dot_general(a, b, dims, preferred_element_type=F32)


def halves(x):
    high = x.astype(BF16)
    return high, (x - high.astype(F32)).astype(BF16)


def dot_wide(a, b, dims=NN):
    a_high, a_low = halves(a)
    b_high, b_low = halves(b)
    return dot(a_high, b_high, dims) + (dot(a_high, b_low, dims) + dot(a_low, b_high, dims))


def power_scale(peak, root=False):
    scale = jnp.ones_like(peak)
    full = jnp.ones_like(peak)
    for exponent in (64, 32, 16, 8, 4, 2, 1):
        big = peak * full >= 2.0**exponent
        full = jnp.where(big, full * 2.0**-exponent, full)
        scale = jnp.where(big, scale * 2.0 ** -(exponent // 2), scale)
    for exponent in (64, 32, 16, 8, 4, 2, 1):
        small = peak * full * 2.0**exponent < 2.0
        full = jnp.where(small, full * 2.0**exponent, full)
        scale = jnp.where(small, scale * 2.0 ** (exponent // 2), scale)
    return scale if root else full


def inverse_factor(gram, work):
    rank = gram.shape[0]
    index = lax.broadcasted_iota(jnp.int32, (rank, 1), 0)
    lane = lax.broadcasted_iota(jnp.int32, (rank, 2 * rank), 1)
    work[:, :rank] = (lax.broadcasted_iota(jnp.int32, (rank, rank), 1) == index).astype(F32)
    work[:, rank:] = gram
    table = work[...]
    for k in range(0, rank, 2):
        at = rank + k
        row, next_row = table[k:k + 1, :], table[k + 1:k + 2, :]
        inverse = 1.0 / row[:, at:at + 1]
        link = row[:, at + 1:at + 2] * inverse
        next_inverse = 1.0 / (next_row[:, at + 1:at + 2] - row[:, at + 1:at + 2] * link)
        column, next_column = table[:, at:at + 1], table[:, at + 1:at + 2]
        factor = jnp.where(index > k, column * inverse, 0.0)
        next_factor = jnp.where(index > k + 1, (next_column - column * link) * next_inverse, 0.0)
        table = table - (factor * row + next_factor * (next_row - link * row))
    pivots = jnp.sum(jnp.where(lane == index + rank, table, 0.0), axis=1, keepdims=True)
    work[...] = table * lax.rsqrt(pivots)
    return work[:, :rank]


def slot_columns(place, gap, width):
    return pl.ds(pl.multiple_of((place ^ gap) * width, 128), width)


def start_pieces(place, gaps, delta_hbm, delta, sems):
    rows, width = delta.shape[1:]
    blocks = sems.shape[1]
    size = rows // blocks
    copies = []
    for number, gap in enumerate(gaps):
        copies.append([])
        for block in range(blocks):
            span = pl.ds(block * size, size)
            copy = pltpu.make_async_copy(
                delta_hbm.at[span, slot_columns(place, gap, width)], delta.at[number, span, :], sems.at[number, block]
            )
            copy.start()
            copies[-1].append(copy)
    return copies


def add_products(copies, delta, pieces, part):
    rows = delta.shape[1]
    size = rows // len(copies[0])
    for number, piece in enumerate(pieces):
        for block, copy in enumerate(copies[number]):
            copy.wait()
            span = slice(block * size, (block + 1) * size)
            part[:, span] += jnp.transpose(dot(delta[number, span, :], piece[...], NT))


def part_kernel(gaps, fresh, place_ref, delta_hbm, *refs):
    pieces = refs[:len(gaps)]
    before, out, delta, sems = refs[len(gaps):] if not fresh else (None, *refs[len(gaps):])
    copies = start_pieces(place_ref[0], gaps, delta_hbm, delta, sems)
    out[...] = jnp.zeros_like(out) if fresh else before[...]
    add_products(copies, delta, pieces, out)


def biggest(pieces):
    peak = None
    for piece in pieces:
        most = jnp.max(jnp.abs(piece[...]).astype(F32), keepdims=True)
        peak = most if peak is None else jnp.maximum(peak, most)
    return peak


def first_kernel(gaps, count, place_ref, delta_hbm, *refs):
    pieces = refs[:count]
    before, out, part, delta, sems = refs[count:]
    copies = start_pieces(place_ref[0], gaps, delta_hbm, delta, sems)
    part[...] = before[...]
    scale = power_scale(biggest(pieces)) * LIFT
    add_products(copies, delta, [pieces[gap] for gap in gaps], part)
    out[...] = (part[...] * scale).astype(BF16)


def second_kernel(gaps, count, place_ref, delta_hbm, *refs):
    pieces = refs[:count]
    before, out, gram, part, delta, sems, work = refs[count:]
    copies = start_pieces(place_ref[0], gaps, delta_hbm, delta, sems)
    part[...] = before[...]
    peak = biggest(pieces)
    scale = power_scale(peak)
    second = power_scale(peak * (1.0 / LIFT), root=True)
    right_gram = None
    for piece in pieces:
        scaled = (piece[...].astype(F32) * scale).astype(BF16)
        term = dot(scaled, scaled, NT)
        right_gram = term if right_gram is None else right_gram + term
    inverse = inverse_factor(right_gram, work) * second
    add_products(copies, delta, [pieces[gap] for gap in gaps], part)
    left = dot_wide(inverse, part[...] * scale).astype(BF16)
    out[...] = left
    gram[...] = dot(left, left, NT)


def delta_call(kernel, place, changes, gaps, args, width, out_shape, scratch, name):
    rows = changes.shape[0]
    vmem = pl.BlockSpec(memory_space=pltpu.VMEM)
    blocks = max(1, rows // 256)
    return pl.pallas_call(
        kernel,
        in_specs=[pl.BlockSpec(memory_space=pltpu.SMEM), pl.BlockSpec(memory_space=pl.ANY)] + [vmem] * len(args),
        out_specs=[vmem] * len(out_shape),
        out_shape=out_shape,
        scratch_shapes=scratch[:1] + [
            pltpu.VMEM((len(gaps), rows, width), BF16), pltpu.SemaphoreType.DMA((len(gaps), blocks))
        ] + scratch[1:],
        compiler_params=pltpu.CompilerParams(vmem_limit_bytes=VMEM_BYTES),
        name=name,
    )(place, changes, *args)


def left_sweep(kernel, place, changes, pieces, out_shape, scratch, name):
    rows = changes.shape[0]
    rank, width = pieces[0].shape
    count = len(pieces)
    part_shape = [jax.ShapeDtypeStruct((rank, rows), F32)]
    split = max(1, count // 4)
    groups = [tuple(range(at, at + split)) for at in range(0, count, split)]
    order = [groups[0], groups[-1]] if len(groups) > 2 else [groups[0]]
    last = tuple(gap for group in groups for gap in group if group not in order)
    part = None
    for gaps in order:
        fresh = part is None
        (part,) = delta_call(
            functools.partial(part_kernel, gaps, fresh), place, changes, gaps,
            [pieces[gap] for gap in gaps] + ([] if fresh else [part]), width, part_shape, [], name + "_part",
        )
    return delta_call(
        functools.partial(kernel, last, count), place, changes, last, [*pieces, part], width, out_shape,
        [pltpu.VMEM((rank, rows), F32)] + scratch, name,
    )


def right_kernel_first(gap, place_ref, delta_hbm, left, out, delta, sems):
    chunks, _, size = delta.shape
    base = (place_ref[0] ^ gap) * (chunks * size)
    copies = [
        pltpu.make_async_copy(
            delta_hbm.at[:, pl.ds(pl.multiple_of(base + chunk * size, 128), size)], delta.at[chunk], sems.at[chunk]
        )
        for chunk in range(chunks)
    ]
    for copy in copies:
        copy.start()
    for chunk, copy in enumerate(copies):
        copy.wait()
        out[:, chunk * size:(chunk + 1) * size] = dot(left[...], delta[chunk]).astype(BF16)


def right_kernel_second(gap, real, place_ref, delta_hbm, left, out, delta, sems):
    groups, _, size = delta.shape
    slot = place_ref[0] ^ gap
    start = slot_start(slot, size, real)
    copies = [
        pltpu.make_async_copy(
            delta_hbm.at[:, pl.ds(pl.multiple_of(group * real + start, 128), size)], delta.at[group], sems.at[group]
        )
        for group in range(groups)
    ]
    for copy in copies:
        copy.start()
    inside = lax.broadcasted_iota(jnp.int32, (1, size), 1) + start >= slot * size
    for group, copy in enumerate(copies):
        copy.wait()
        out[group] = jnp.where(inside, dot(left[...], delta[group]), 0.0).astype(BF16)


def slot_start(slot, size, real):
    return jnp.minimum(slot * size, real - size)


def right_call(kernel, place, changes, left, chunks, size, out_shape, name):
    vmem = pl.BlockSpec(memory_space=pltpu.VMEM)
    return pl.pallas_call(
        kernel,
        in_specs=[pl.BlockSpec(memory_space=pltpu.SMEM), pl.BlockSpec(memory_space=pl.ANY), vmem],
        out_specs=vmem,
        out_shape=out_shape,
        scratch_shapes=[pltpu.VMEM((chunks, changes.shape[0], size), BF16), pltpu.SemaphoreType.DMA((chunks,))],
        compiler_params=pltpu.CompilerParams(vmem_limit_bytes=VMEM_BYTES),
        name=name,
    )(place, changes, left)


def small_call(kernel, out_shape, args, scratch=(), name=None, scalars=0):
    spec = lambda i: pl.BlockSpec(memory_space=pltpu.SMEM if i < scalars else pltpu.VMEM)
    return pl.pallas_call(
        kernel,
        in_specs=[spec(i) for i in range(len(args))],
        out_specs=[pl.BlockSpec(memory_space=pltpu.VMEM)] * len(out_shape),
        out_shape=out_shape,
        scratch_shapes=list(scratch),
        compiler_params=pltpu.CompilerParams(vmem_limit_bytes=VMEM_BYTES),
        name=name,
    )(*args)


def left_kernel(count, left, *refs):
    grams, (out, inverse, work) = refs[:count], refs[count:]
    total = grams[0][...]
    for gram in grams[1:]:
        total = total + gram[...]
    factor = inverse_factor(total, work)
    inverse[...] = factor
    high, low = halves(factor)
    out[...] = (dot(high, left[...]) + dot(low, left[...])).astype(BF16)


def right_sum_kernel(count, *refs):
    parts, (total, gram) = refs[:count], refs[count:]
    result = None
    for group in range(total.shape[0]):
        value = parts[0][group].astype(F32)
        for part in parts[1:]:
            value = value + part[group].astype(F32)
        total[group] = value
        term = dot_wide(value, value, NT)
        result = term if result is None else result + term
    gram[...] = result


def right_kernel(count, groups, place_ref, weight_ref, total, left_inverse, *refs):
    grams, outs, (work,) = refs[:count], refs[count:count + groups], refs[count + groups:]
    gram = grams[0][...]
    for other in grams[1:]:
        gram = gram + other[...]
    factor = inverse_factor(gram, work)
    middle_high, middle_low = halves(weight_ref[0] * dot_wide(left_inverse[...], dot_wide(gram, factor, NT)))
    high, low = halves(factor)
    rank, size = total.shape[1:]
    for gap, out in enumerate(outs):
        value_high, value_low = halves(total[place_ref[0] ^ gap])
        out[:, :size] = (dot(high, value_high) + (dot(high, value_low) + dot(low, value_high))).astype(BF16)
        out[:, size:size + rank] = middle_high
        out[:, size + rank:] = middle_low


def right_gram_kernel(groups, place_ref, *refs):
    pieces, (stack, middles, home, away) = refs[:groups], refs[groups:]
    rank = pieces[0].shape[0]
    size = stack.shape[1]
    place = place_ref[0]
    for gap, piece in enumerate(pieces):
        owner = place ^ gap
        stack[pl.ds(pl.multiple_of(owner * rank, rank), rank), :] = piece[:, :size]
        middles[owner] = piece[:, size:size + rank].astype(F32) + piece[:, size + rank:].astype(F32)
    for number in range(groups // 2):
        for out, gap in ((home, 2 * number), (away, 2 * number + 1)):
            at = pl.multiple_of((place ^ gap) * rank, rank)
            out[number] = dot(stack[pl.ds(at, rank), :], stack[...], NT).astype(BF16)


def left_gram_kernel(place_ref, stack, out):
    rank = out.shape[0]
    at = pl.multiple_of(place_ref[0] * rank, rank)
    out[...] = dot(stack[pl.ds(at, rank), :], stack[...], NT).astype(BF16)


def fill_gram(place, pairs, gram):
    rank = pairs[0].shape[1]
    for number, pair in enumerate(pairs):
        for side in range(2):
            at = pl.multiple_of((place ^ (2 * number + side)) * rank, rank)
            gram[pl.ds(at, rank), :] = pair[side].astype(F32)


def polish(count, gram, product, spare, side):
    size = gram.shape[0]
    strip = min(512, size)
    eye = (
        lax.broadcasted_iota(jnp.int32, (size, size), 0) == lax.broadcasted_iota(jnp.int32, (size, size), 1)
    ).astype(F32)
    lead, tail = 1.5 / math.sqrt(count), -0.5 / (count * math.sqrt(count))
    product[...] = lead * eye + tail * gram[...]

    def multiply(a_ref, c_ref, lead, tail):
        def one(index, _):
            rows = pl.ds(pl.multiple_of(index * strip, strip), strip)
            a = a_ref[rows, :]
            c_ref[rows, :] = lead * a + tail * dot(a.astype(BF16), side[...])
            return 0

        lax.fori_loop(0, size // strip, one, 0)

    def step(index, _):
        first = index == 1
        before = jnp.where(first, lead, 1.5)
        after = jnp.where(first, tail, -0.5)
        side[...] = gram[...].astype(BF16)
        multiply(gram, spare, before, after)
        multiply(spare, gram, before, after)
        side[...] = gram[...].astype(BF16)
        multiply(product, product, 1.5, -0.5)
        return 0

    lax.fori_loop(1, NS_ITERS, step, 0)


def left_mix_kernel(count, place_ref, *refs):
    pairs, (stack, middle, out, gram, product, spare, side) = refs[:count // 2], refs[count // 2:]
    fill_gram(place_ref[0], pairs, gram)
    polish(count, gram, product, spare, side)
    rank = middle.shape[1]
    for index in range(count):
        rows = pl.ds(index * rank, rank)
        spare[rows, :] = dot_wide(jnp.transpose(middle[index]), product[rows, :])
    side[...] = spare[...].astype(BF16)
    out[...] = dot(side[...], stack[...]).astype(BF16)


def merge_kernel(count, ckpt_count, places_ref, mixed, *refs):
    pairs, refs = refs[:ckpt_count // 2], refs[ckpt_count // 2:]
    pieces, (out, gram, product, spare, side, wide) = refs[:count], refs[count:]
    real = out.shape[1]

    @pl.when(pl.program_id(0) == 0)
    def _():
        fill_gram(places_ref[0], pairs, gram)
        size = pieces[0].shape[1]
        wide[...] = jnp.zeros_like(wide)
        for gap, piece in enumerate(pieces):
            start = pl.multiple_of(slot_start(places_ref[1] ^ gap, size, real), 128)
            wide[:, pl.ds(start, size)] += piece[...]
        polish(ckpt_count, gram, product, spare, side)
        side[...] = product[...].astype(BF16)

    turned = jnp.transpose(dot(side[...], mixed[...])).astype(BF16)
    out[...] = dot(turned, wide[...]).astype(BF16)


def permute(value, axis, gap):
    count = lax.axis_size(axis)
    return lax.ppermute(value, axis, [(source, source ^ gap) for source in range(count)])


def spread(value, axis):
    return [value] + [permute(value, axis, gap) for gap in range(1, lax.axis_size(axis))]


def swap(values, axis):
    return [values[0]] + [permute(value, axis, gap) for gap, value in enumerate(values) if gap]


def spread_pairs(value):
    pair = jnp.stack([value, permute(value, "ckpt", 1)])
    return [pair] + [permute(pair, "ckpt", gap) for gap in range(2, lax.axis_size("ckpt"), 2)]


def add_up(values):
    return sum(value.astype(F32) for value in values)


def body(deltas, start_basis, edit_order):
    changes = deltas[0]
    start = jnp.transpose(start_basis[0])
    rank, width = start.shape
    rows, cols = changes.shape
    count = lax.axis_size("rows")
    groups = lax.axis_size("ckpt")
    row_place = lax.axis_index("rows").astype(jnp.int32)
    ckpt_place = lax.axis_index("ckpt").astype(jnp.int32)
    at_row = row_place[None]
    at_ckpt = ckpt_place[None]
    at_both = jnp.stack([ckpt_place, row_place])
    shape = jax.ShapeDtypeStruct
    square = shape((rank, rank), F32)
    work = pltpu.VMEM((rank, 2 * rank), F32)
    remote_first = list(range(count - 1, 0, -1)) + [0]

    (left,) = left_sweep(
        first_kernel, at_row, changes, spread(start, "rows"), [shape((rank, rows), BF16)], [], "first_left"
    )
    chunk = width // 4 if width % 512 == 0 else width
    parts = [None] * count
    for gap in remote_first:
        piece = right_call(
            functools.partial(right_kernel_first, gap), at_row, changes, left, width // chunk, chunk,
            shape((rank, width), BF16), "first_right",
        )
        parts[gap] = permute(piece, "rows", gap) if gap else piece
    right = add_up(parts).astype(BF16)

    block = cols // groups
    padded = -(-block // (count * 128)) * 128
    left, left_gram = left_sweep(
        second_kernel, at_row, changes, spread(right, "rows"), [shape((rank, rows), BF16), square], [work],
        "second_left",
    )
    left_grams = spread(left_gram, "rows")
    for gap in remote_first:
        piece = right_call(
            functools.partial(right_kernel_second, gap, block), at_row, changes, left, groups, padded,
            shape((groups, rank, padded), BF16), "second_right",
        )
        parts[gap] = permute(piece, "rows", gap) if gap else piece

    left_unit, left_inverse = small_call(
        functools.partial(left_kernel, count), [shape((rank, rows), BF16), square],
        [left] + left_grams, [work], "left_unit",
    )
    left_stack = lax.all_gather(left_unit, "ckpt", axis=0, tiled=True)

    total, right_gram = small_call(
        functools.partial(right_sum_kernel, count), [shape((groups, rank, padded), F32), square], parts,
        name="right_sum",
    )
    position = jnp.sum(jnp.where(jnp.arange(groups) == ckpt_place, edit_order, 0))
    weight = (1 + position).astype(F32)[None] / groups
    leaving = small_call(
        functools.partial(right_kernel, count, groups), [shape((rank, padded + 2 * rank), BF16)] * groups,
        [at_ckpt, weight, total, left_inverse] + spread(right_gram, "rows"), [work], "right_unit", scalars=2,
    )
    pieces = swap(leaving, "ckpt")

    size = groups * rank
    (left_rows,) = small_call(left_gram_kernel, [shape((rank, size), BF16)], [at_ckpt, left_stack], name="left_gram",
                              scalars=1)
    left_pairs = spread_pairs(add_up(spread(left_rows, "rows")).astype(BF16))

    table = pltpu.VMEM((size, size), F32)
    tables = [table, table, table, pltpu.VMEM((size, size), BF16)]
    slabs = shape((groups // 2, rank, size), BF16)
    right_stack, middles, home, away = small_call(
        functools.partial(right_gram_kernel, groups),
        [shape((size, padded), BF16), shape((groups, rank, rank), F32), slabs, slabs],
        [at_ckpt] + pieces, name="right_gram", scalars=1,
    )
    right_all = spread(right_stack, "rows")
    pair_sum = add_up([home, permute(away, "ckpt", 1)]).astype(BF16)
    own = add_up([pair_sum[0]] + [permute(pair_sum[n], "ckpt", 2 * n) for n in range(1, groups // 2)]).astype(BF16)
    right_pairs = spread_pairs(add_up(spread(own, "rows")).astype(BF16))

    (mixed,) = small_call(
        functools.partial(left_mix_kernel, groups), [shape((size, rows), BF16)],
        [at_ckpt] + left_pairs + [left_stack, middles], tables, "left_mix", scalars=1,
    )
    step = min(512, rows)
    full = lambda value: pl.BlockSpec(value.shape, lambda i: (0,) * value.ndim)
    return pl.pallas_call(
        functools.partial(merge_kernel, count, groups),
        grid=(rows // step,),
        in_specs=[pl.BlockSpec(memory_space=pltpu.SMEM), pl.BlockSpec((size, step), lambda i: (0, i))]
        + [full(value) for value in right_pairs + right_all],
        out_specs=pl.BlockSpec((step, block), lambda i: (i, 0)),
        out_shape=shape((rows, block), BF16),
        scratch_shapes=tables + [pltpu.VMEM((size, block), BF16)],
        compiler_params=pltpu.CompilerParams(vmem_limit_bytes=VMEM_BYTES),
        name="merge",
    )(at_both, mixed, *right_pairs, *right_all)


def solution(mesh):
    return jax.shard_map(
        body,
        mesh=mesh,
        in_specs=(P("ckpt", "rows", None), P("ckpt", "rows", None), P()),
        out_specs=P("rows", "ckpt"),
        check_vma=False,
    )
```

```python
import functools
import math

import jax
import jax.numpy as jnp
from jax import lax
from jax.experimental import pallas as pl
from jax.experimental.pallas import tpu as pltpu
from jax.sharding import PartitionSpec as P

NS_ITERS = 4
LIFT = 2.0**60
VMEM_BYTES = 56 * 1024 * 1024
SHORT = pl.CostEstimate(flops=1024, bytes_accessed=1024, transcendentals=0)
F32 = jnp.float32
BF16 = jnp.bfloat16
NN = (((1,), (0,)), ((), ()))
NT = (((1,), (1,)), ((), ()))
TN = (((0,), (0,)), ((), ()))


def dot(a, b, dims=NN):
    return lax.dot_general(a, b, dims, preferred_element_type=F32)


def halves(x):
    high = x.astype(BF16)
    return high, (x - high.astype(F32)).astype(BF16)


def dot_wide(a, b, dims=NN):
    a_high, a_low = halves(a)
    b_high, b_low = halves(b)
    return dot(a_high, b_high, dims) + (dot(a_high, b_low, dims) + dot(a_low, b_high, dims))


def power_scale(peak, root=False):
    scale = jnp.ones_like(peak)
    full = jnp.ones_like(peak)
    for exponent in (64, 32, 16, 8, 4, 2, 1):
        big = peak * full >= 2.0**exponent
        full = jnp.where(big, full * 2.0**-exponent, full)
        scale = jnp.where(big, scale * 2.0 ** -(exponent // 2), scale)
    for exponent in (64, 32, 16, 8, 4, 2, 1):
        small = peak * full * 2.0**exponent < 2.0
        full = jnp.where(small, full * 2.0**exponent, full)
        scale = jnp.where(small, scale * 2.0 ** (exponent // 2), scale)
    return scale if root else full


def inverse_factor(gram, work):
    rank = gram.shape[0]
    index = lax.broadcasted_iota(jnp.int32, (rank, 1), 0)
    lane = lax.broadcasted_iota(jnp.int32, (rank, 2 * rank), 1)
    work[:, :rank] = (lax.broadcasted_iota(jnp.int32, (rank, rank), 1) == index).astype(F32)
    work[:, rank:] = gram
    tiles = [work[at:at + 8, :] for at in range(0, rank, 8)]
    below = lax.broadcasted_iota(jnp.int32, (8, 1), 0)
    for k in range(rank - 1):
        at = rank + k
        first, inner = divmod(k, 8)
        row = tiles[first][inner:inner + 1, :]
        row = row * (1.0 / row[:, at:at + 1])
        for number in range(first, len(tiles)):
            column = tiles[number][:, at:at + 1]
            if number == first:
                column = jnp.where(below > inner, column, 0.0)
            tiles[number] = tiles[number] - column * row
    table = jnp.concatenate(tiles, axis=0)
    pivots = jnp.sum(jnp.where(lane == index + rank, table, 0.0), axis=1, keepdims=True)
    work[...] = table * lax.rsqrt(pivots)
    return work[:, :rank]


def slot_columns(place, gap, width):
    return pl.ds(pl.multiple_of((place ^ gap) * width, 128), width)


def start_pieces(place, gaps, delta_hbm, delta, sems):
    rows, width = delta.shape[1:]
    blocks = sems.shape[1]
    size = rows // blocks
    copies = []
    for number, gap in enumerate(gaps):
        copies.append([])
        for block in range(blocks):
            span = pl.ds(block * size, size)
            copy = pltpu.make_async_copy(
                delta_hbm.at[span, slot_columns(place, gap, width)], delta.at[number, span, :], sems.at[number, block]
            )
            copy.start()
            copies[-1].append(copy)
    return copies


def add_products(copies, delta, pieces, part):
    rows = delta.shape[1]
    size = rows // len(copies[0])
    block = min(256, rows)
    for number, piece in enumerate(pieces):
        for start in range(0, rows, block):
            for copy in copies[number][start // size:(start + block) // size]:
                copy.wait()
            part[:, start:start + block] += dot(piece[...], delta[number, start:start + block, :], NT)


def part_kernel(gaps, fresh, place_ref, delta_hbm, *refs):
    pieces = refs[:len(gaps)]
    before, out, delta, sems = refs[len(gaps):] if not fresh else (None, *refs[len(gaps):])
    copies = start_pieces(place_ref[0], gaps, delta_hbm, delta, sems)
    out[...] = jnp.zeros_like(out) if fresh else before[...]
    add_products(copies, delta, pieces, out)


def biggest(pieces):
    peak = None
    for piece in pieces:
        most = jnp.max(jnp.abs(piece[...]).astype(F32), keepdims=True)
        peak = most if peak is None else jnp.maximum(peak, most)
    return peak


def first_kernel(gaps, count, place_ref, delta_hbm, *refs):
    pieces = refs[:count]
    before, out, part, delta, sems = refs[count:]
    copies = start_pieces(place_ref[0], gaps, delta_hbm, delta, sems)
    part[...] = before[...]
    scale = power_scale(biggest(pieces)) * LIFT
    add_products(copies, delta, [pieces[gap] for gap in gaps], part)
    out[...] = (part[...] * scale).astype(BF16)


def second_kernel(gaps, count, place_ref, delta_hbm, *refs):
    pieces = refs[:count]
    before, out, gram, part, delta, sems, work = refs[count:]
    copies = start_pieces(place_ref[0], gaps, delta_hbm, delta, sems)
    part[...] = before[...]
    peak = biggest(pieces)
    scale = power_scale(peak)
    second = power_scale(peak * (1.0 / LIFT), root=True)
    right_gram = None
    for piece in pieces:
        scaled = (piece[...].astype(F32) * scale).astype(BF16)
        term = dot(scaled, scaled, NT)
        right_gram = term if right_gram is None else right_gram + term
    inverse = inverse_factor(right_gram, work) * second
    add_products(copies, delta, [pieces[gap] for gap in gaps], part)
    left = dot_wide(inverse, part[...] * scale).astype(BF16)
    out[...] = left
    gram[...] = dot(left, left, NT)


def delta_call(kernel, place, changes, gaps, args, width, out_shape, scratch, name):
    rows = changes.shape[0]
    vmem = pl.BlockSpec(memory_space=pltpu.VMEM)
    blocks = max(1, rows // 128)
    return pl.pallas_call(
        kernel,
        in_specs=[pl.BlockSpec(memory_space=pltpu.SMEM), pl.BlockSpec(memory_space=pl.ANY)] + [vmem] * len(args),
        out_specs=[vmem] * len(out_shape),
        out_shape=out_shape,
        scratch_shapes=scratch[:1] + [
            pltpu.VMEM((len(gaps), rows, width), BF16), pltpu.SemaphoreType.DMA((len(gaps), blocks))
        ] + scratch[1:],
        compiler_params=pltpu.CompilerParams(vmem_limit_bytes=VMEM_BYTES),
        name=name,
        cost_estimate=SHORT,
    )(place, changes, *args)


def left_sweep(kernel, place, changes, own, out_shape, scratch, name):
    rows = changes.shape[0]
    rank, width = own.shape
    count = lax.axis_size("rows")
    part_shape = [jax.ShapeDtypeStruct((rank, rows), F32)]
    near = tuple(gap for gap in range(1, count) if not gap & (gap - 1))
    far = tuple(gap for gap in range(1, count) if gap & (gap - 1))

    def add(gaps, args):
        return delta_call(
            functools.partial(part_kernel, gaps, gaps == (0,)), place, changes, gaps, args, width, part_shape, [],
            name + "_part",
        )[0]

    arrived = [permute(own, "rows", gap) for gap in near]
    part, *arrived = together(add((0,), [own]), *arrived)
    pieces = [own] + [None] * (count - 1)
    for gap, piece in zip(near, arrived):
        pieces[gap] = piece
    forward(pieces, "rows")
    if far:
        part = add(near, [*arrived, part])
    last = far or near
    return delta_call(
        functools.partial(kernel, last, count), place, changes, last, [*pieces, part], width, out_shape,
        [pltpu.VMEM((rank, rows), F32)] + scratch, name,
    )


def start_columns(delta_hbm, starts, delta, sems):
    chunks, rows, size = delta.shape
    blocks = sems.shape[1]
    copies = []
    for chunk, start in enumerate(starts):
        copies.append([])
        for block in range(blocks):
            span = pl.ds(block * (rows // blocks), rows // blocks)
            copy = pltpu.make_async_copy(
                delta_hbm.at[span, pl.ds(pl.multiple_of(start, 128), size)], delta.at[chunk, span, :],
                sems.at[chunk, block],
            )
            copy.start()
            copies[-1].append(copy)
    return copies


def right_kernel_first(gap, place_ref, delta_hbm, left, out, delta, sems):
    chunks, _, size = delta.shape
    base = (place_ref[0] ^ gap) * (chunks * size)
    copies = start_columns(delta_hbm, [base + chunk * size for chunk in range(chunks)], delta, sems)
    for chunk, group in enumerate(copies):
        for copy in group:
            copy.wait()
        out[:, chunk * size:(chunk + 1) * size] = dot(left[...], delta[chunk]).astype(BF16)


def right_kernel_second(gap, real, place_ref, delta_hbm, left, out, delta, sems):
    groups, _, size = delta.shape
    slot = place_ref[0] ^ gap
    start = slot_start(slot, size, real)
    copies = start_columns(delta_hbm, [group * real + start for group in range(groups)], delta, sems)
    inside = lax.broadcasted_iota(jnp.int32, (1, size), 1) + start >= slot * size
    for group, parts in enumerate(copies):
        for copy in parts:
            copy.wait()
        out[group] = jnp.where(inside, dot(left[...], delta[group]), 0.0).astype(BF16)


def own_kernel_second(count, real, place_ref, delta_hbm, left, *refs):
    grams, (out, unit, inverse, delta, sems, work) = refs[:count], refs[count:]
    right_kernel_second(0, real, place_ref, delta_hbm, left, out, delta, sems)
    total = grams[0][...]
    for gram in grams[1:]:
        total = total + gram[...]
    factor = inverse_factor(total, work)
    inverse[...] = factor
    high, low = halves(factor)
    unit[...] = (dot(high, left[...]) + dot(low, left[...])).astype(BF16)


def slot_start(slot, size, real):
    return jnp.minimum(slot * size, real - size)


def right_call(kernel, place, changes, args, chunks, size, out_shape, name, scratch=()):
    rows = changes.shape[0]
    vmem = pl.BlockSpec(memory_space=pltpu.VMEM)
    return pl.pallas_call(
        kernel,
        in_specs=[pl.BlockSpec(memory_space=pltpu.SMEM), pl.BlockSpec(memory_space=pl.ANY)] + [vmem] * len(args),
        out_specs=[vmem] * len(out_shape),
        out_shape=out_shape,
        scratch_shapes=[pltpu.VMEM((chunks, rows, size), BF16),
                        pltpu.SemaphoreType.DMA((chunks, max(1, rows // 256))), *scratch],
        compiler_params=pltpu.CompilerParams(vmem_limit_bytes=VMEM_BYTES),
        name=name,
        cost_estimate=SHORT,
    )(place, changes, *args)


def small_call(kernel, out_shape, args, scratch=(), name=None, scalars=0):
    spec = lambda i: pl.BlockSpec(memory_space=pltpu.SMEM if i < scalars else pltpu.VMEM)
    return pl.pallas_call(
        kernel,
        in_specs=[spec(i) for i in range(len(args))],
        out_specs=[pl.BlockSpec(memory_space=pltpu.VMEM)] * len(out_shape),
        out_shape=out_shape,
        scratch_shapes=list(scratch),
        compiler_params=pltpu.CompilerParams(vmem_limit_bytes=VMEM_BYTES),
        name=name,
        cost_estimate=SHORT,
    )(*args)


def right_sum_kernel(count, *refs):
    parts, (total, gram) = refs[:count], refs[count:]
    result = None
    for group in range(total.shape[0]):
        value = parts[0][group].astype(F32)
        for part in parts[1:]:
            value = value + part[group].astype(F32)
        total[group] = value
        term = dot_wide(value, value, NT)
        result = term if result is None else result + term
    gram[...] = result


def right_kernel(count, groups, place_ref, weight_ref, total, left_inverse, *refs):
    grams, outs, (work,) = refs[:count], refs[count:count + groups], refs[count + groups:]
    gram = grams[0][...]
    for other in grams[1:]:
        gram = gram + other[...]
    factor = inverse_factor(gram, work)
    middle_high, middle_low = halves(weight_ref[0] * dot_wide(left_inverse[...], dot_wide(gram, factor, NT)))
    high, low = halves(factor)
    rank, size = total.shape[1:]
    for gap, out in enumerate(outs):
        value_high, value_low = halves(total[place_ref[0] ^ gap])
        out[:, :size] = (dot(high, value_high) + (dot(high, value_low) + dot(low, value_high))).astype(BF16)
        out[:, size:size + rank] = middle_high
        out[:, size + rank:] = middle_low


def grams_kernel(groups, place_ref, left_stack, *refs):
    pieces, (stack, middles, home, away, *slabs) = refs[:groups], refs[groups:]
    left_rows = slabs[0].shape[0]
    for gap, slab in enumerate(slabs):
        at = pl.multiple_of((place_ref[1] ^ gap) * left_rows, left_rows)
        slab[...] = dot(left_stack[pl.ds(at, left_rows), :], left_stack[...], NT).astype(BF16)
    rank = pieces[0].shape[0]
    size = stack.shape[1]
    place = place_ref[0]
    for gap, piece in enumerate(pieces):
        owner = place ^ gap
        stack[pl.ds(pl.multiple_of(owner * rank, rank), rank), :] = piece[:, :size]
        middles[owner] = piece[:, size:size + rank].astype(F32) + piece[:, size + rank:].astype(F32)
    for number in range(groups // 2):
        for out, gap in ((home, 2 * number), (away, 2 * number + 1)):
            at = pl.multiple_of((place ^ gap) * rank, rank)
            out[number] = dot(stack[pl.ds(at, rank), :], stack[...], NT).astype(BF16)


def fill_gram(place, pairs, gram):
    rank = pairs[0].shape[1]
    for number, pair in enumerate(pairs):
        for side in range(2):
            at = pl.multiple_of((place ^ (2 * number + side)) * rank, rank)
            gram[pl.ds(at, rank), :] = pair[side].astype(F32)


def polish(count, gram, product, spare, side):
    size = gram.shape[0]
    strip = min(512, size)
    eye = (
        lax.broadcasted_iota(jnp.int32, (size, size), 0) == lax.broadcasted_iota(jnp.int32, (size, size), 1)
    ).astype(F32)
    lead, tail = 1.5 / math.sqrt(count), -0.5 / (count * math.sqrt(count))
    product[...] = lead * eye + tail * gram[...]

    def multiply(a_ref, c_ref, lead, tail):
        def one(index, _):
            rows = pl.ds(pl.multiple_of(index * strip, strip), strip)
            a = a_ref[rows, :]
            c_ref[rows, :] = lead * a + tail * dot(a.astype(BF16), side[...])
            return 0

        lax.fori_loop(0, size // strip, one, 0)

    def step(index, _):
        first = index == 1
        before = jnp.where(first, lead, 1.5)
        after = jnp.where(first, tail, -0.5)
        side[...] = gram[...].astype(BF16)
        multiply(gram, spare, before, after)
        multiply(spare, gram, before, after)
        side[...] = gram[...].astype(BF16)
        multiply(product, product, 1.5, -0.5)
        return 0

    lax.fori_loop(1, NS_ITERS, step, 0)


def left_mix_kernel(count, ckpt_count, place_ref, *refs):
    slabs, (stack, middle, out, gram, product, spare, side) = refs[:count], refs[count:]
    slab_rows = slabs[0].shape[0]
    for gap, slab in enumerate(slabs):
        at = pl.multiple_of((place_ref[0] ^ gap) * slab_rows, slab_rows)
        gram[pl.ds(at, slab_rows), :] = slab[...].astype(F32)
    polish(ckpt_count, gram, product, spare, side)
    rank = middle.shape[1]
    for index in range(ckpt_count):
        rows = pl.ds(index * rank, rank)
        spare[rows, :] = dot_wide(jnp.transpose(middle[index]), product[rows, :])
    side[...] = spare[...].astype(BF16)
    out[...] = dot(side[...], stack[...]).astype(BF16)


def merge_kernel(count, ckpt_count, places_ref, mixed, *refs):
    pairs, refs = refs[:ckpt_count // 2], refs[ckpt_count // 2:]
    pieces, (out, gram, product, spare, side, wide) = refs[:count], refs[count:]
    real = out.shape[1]

    @pl.when(pl.program_id(0) == 0)
    def _():
        fill_gram(places_ref[0], pairs, gram)
        size = pieces[0].shape[1]
        wide[...] = jnp.zeros_like(wide)
        for gap, piece in enumerate(pieces):
            start = pl.multiple_of(slot_start(places_ref[1] ^ gap, size, real), 128)
            wide[:, pl.ds(start, size)] += piece[...]
        polish(ckpt_count, gram, product, spare, side)
        side[...] = product[...].astype(BF16)

    turned = jnp.transpose(dot(side[...], mixed[...])).astype(BF16)
    out[...] = dot(turned, wide[...]).astype(BF16)


def permute(value, axis, gap):
    count = lax.axis_size(axis)
    return lax.ppermute(value, axis, [(source, source ^ gap) for source in range(count)])


def spread(value, axis):
    return [value] + [permute(value, axis, gap) for gap in range(1, lax.axis_size(axis))]


def forward(got, axis):
    half = got[0].shape[0] // 2
    for gap in sorted(range(1, len(got)), key=lambda gap: bin(gap).count("1")):
        low, high = gap & -gap, 1 << (gap.bit_length() - 1)
        if low != high:
            got[gap] = jnp.concatenate([
                permute(got[gap ^ low][:half], axis, low), permute(got[gap ^ high][half:], axis, high)
            ])
    return got


def spread_twice(value, axis):
    got = [value] + [None if gap & (gap - 1) else permute(value, axis, gap) for gap in range(1, lax.axis_size(axis))]
    return forward(got, axis)


def swap(values, axis):
    return [values[0]] + [permute(value, axis, gap) for gap, value in enumerate(values) if gap]


def right_sweep(call, left, count, small=()):
    parts = [None] * count
    for gap in range(count - 1, 0, -1):
        piece, left = together(call(gap, left), left)
        if small:
            left, *small = together(left, *small)
        parts[gap] = permute(piece, "rows", gap)
    if count > 2:
        left, parts[count - 1] = together(left, parts[count - 1])
    parts[0] = call(0, left, *small)
    return parts


def spread_pairs(value):
    pair = jnp.stack([value, permute(value, "ckpt", 1)])
    return [pair] + [permute(pair, "ckpt", gap) for gap in range(2, lax.axis_size("ckpt"), 2)]


def together(*values):
    return lax.optimization_barrier(values)


def add_up(values):
    return sum(value.astype(F32) for value in values)


def body(deltas, start_basis, edit_order):
    changes = deltas[0]
    start = jnp.transpose(start_basis[0])
    rank, width = start.shape
    rows, cols = changes.shape
    count = lax.axis_size("rows")
    groups = lax.axis_size("ckpt")
    row_place = lax.axis_index("rows").astype(jnp.int32)
    ckpt_place = lax.axis_index("ckpt").astype(jnp.int32)
    at_row = row_place[None]
    at_ckpt = ckpt_place[None]
    at_both = jnp.stack([ckpt_place, row_place])
    shape = jax.ShapeDtypeStruct
    square = shape((rank, rank), F32)
    work = pltpu.VMEM((rank, 2 * rank), F32)
    (left,) = left_sweep(
        first_kernel, at_row, changes, start, [shape((rank, rows), BF16)], [], "first_left"
    )
    chunk = 512 if width % 512 == 0 else width
    parts = right_sweep(
        lambda gap, left: right_call(
            functools.partial(right_kernel_first, gap), at_row, changes, [left], width // chunk, chunk,
            [shape((rank, width), BF16)], "first_right",
        )[0],
        left, count,
    )
    right = add_up(parts).astype(BF16)

    block = cols // groups
    padded = -(-block // (count * 128)) * 128
    left, left_gram = left_sweep(
        second_kernel, at_row, changes, right, [shape((rank, rows), BF16), square], [work],
        "second_left",
    )
    left_grams = spread(left_gram, "rows")

    def right_piece(gap, left, *grams):
        if gap:
            return right_call(
                functools.partial(right_kernel_second, gap, block), at_row, changes, [left], groups, padded,
                [shape((groups, rank, padded), BF16)], "second_right",
            )[0]
        return right_call(
            functools.partial(own_kernel_second, count, block), at_row, changes, [left, *grams], groups, padded,
            [shape((groups, rank, padded), BF16), shape((rank, rows), BF16), square], "second_own", [work],
        )

    parts = right_sweep(right_piece, left, count, left_grams)
    parts[0], left_unit, left_inverse = parts[0]
    left_unit, *arrived = together(left_unit, *parts[1:])
    parts[1:] = arrived
    left_stack = lax.all_gather(left_unit, "ckpt", axis=0, tiled=True)
    total, right_gram = small_call(
        functools.partial(right_sum_kernel, count), [shape((groups, rank, padded), F32), square], parts,
        name="right_sum",
    )
    position = jnp.sum(jnp.where(jnp.arange(groups) == ckpt_place, edit_order, 0))
    weight = (1 + position).astype(F32)[None] / groups
    leaving = small_call(
        functools.partial(right_kernel, count, groups), [shape((rank, padded + 2 * rank), BF16)] * groups,
        [at_ckpt, weight, total, left_inverse] + spread(right_gram, "rows"), [work], "right_unit", scalars=2,
    )
    pieces = swap(leaving, "ckpt")
    size = groups * rank
    table = pltpu.VMEM((size, size), F32)
    tables = [table, table, table, pltpu.VMEM((size, size), BF16)]
    slabs = shape((groups // 2, rank, size), BF16)
    right_stack, middles, home, away, *left_slabs = small_call(
        functools.partial(grams_kernel, groups),
        [shape((size, padded), BF16), shape((groups, rank, rank), F32), slabs, slabs]
        + [shape((size // count, size), BF16)] * count,
        [at_both, left_stack] + pieces, name="grams", scalars=1,
    )
    left_slab = add_up(swap(left_slabs, "rows")).astype(BF16)
    pair_sum = add_up([home, permute(away, "ckpt", 1)]).astype(BF16)
    own = add_up([pair_sum[0]] + [permute(pair_sum[n], "ckpt", 2 * n) for n in range(1, groups // 2)]).astype(BF16)
    right_stack, left_slab = together(right_stack, left_slab)
    own, left_slab = together(own, left_slab)
    right_all = spread_twice(right_stack, "rows")
    left_slabs = spread(left_slab, "rows")
    right_pairs = spread_pairs(add_up(spread(own, "rows")).astype(BF16))

    (mixed,) = small_call(
        functools.partial(left_mix_kernel, count, groups), [shape((size, rows), BF16)],
        [at_row] + left_slabs + [left_stack, middles], tables, "left_mix", scalars=1,
    )
    step = min(512, rows)
    full = lambda value: pl.BlockSpec(value.shape, lambda i: (0,) * value.ndim)
    return pl.pallas_call(
        functools.partial(merge_kernel, count, groups),
        grid=(rows // step,),
        in_specs=[pl.BlockSpec(memory_space=pltpu.SMEM), pl.BlockSpec((size, step), lambda i: (0, i))]
        + [full(value) for value in right_pairs + right_all],
        out_specs=pl.BlockSpec((step, block), lambda i: (i, 0)),
        out_shape=shape((rows, block), BF16),
        scratch_shapes=tables + [pltpu.VMEM((size, block), BF16)],
        compiler_params=pltpu.CompilerParams(vmem_limit_bytes=VMEM_BYTES),
        name="merge",
        cost_estimate=SHORT,
    )(at_both, mixed, *right_pairs, *right_all)


def solution(mesh):
    return jax.shard_map(
        body,
        mesh=mesh,
        in_specs=(P("ckpt", "rows", None), P("ckpt", "rows", None), P()),
        out_specs=P("rows", "ckpt"),
        check_vma=False,
    )
```

```python
import functools
import math

import jax
import jax.numpy as jnp
from jax import lax
from jax.experimental import pallas as pl
from jax.experimental.pallas import tpu as pltpu
from jax.sharding import PartitionSpec as P

NS_ITERS = 4
LIFT = 2.0**60
VMEM_BYTES = 24 * 1024 * 1024
DELTA_VMEM_BYTES = 22 * 1024 * 1024
SHORT = pl.CostEstimate(flops=1024, bytes_accessed=1024, transcendentals=0)
F32 = jnp.float32
BF16 = jnp.bfloat16
NN = (((1,), (0,)), ((), ()))
NT = (((1,), (1,)), ((), ()))
TN = (((0,), (0,)), ((), ()))


def dot(a, b, dims=NN):
    return lax.dot_general(a, b, dims, preferred_element_type=F32)


def halves(x):
    high = x.astype(BF16)
    return high, (x - high.astype(F32)).astype(BF16)


def dot_wide(a, b, dims=NN):
    a_high, a_low = halves(a)
    b_high, b_low = halves(b)
    return dot(a_high, b_high, dims) + (dot(a_high, b_low, dims) + dot(a_low, b_high, dims))


def power_scale(peak, root=False):
    scale = jnp.ones_like(peak)
    full = jnp.ones_like(peak)
    for exponent in (64, 32, 16, 8, 4, 2, 1):
        big = peak * full >= 2.0**exponent
        full = jnp.where(big, full * 2.0**-exponent, full)
        scale = jnp.where(big, scale * 2.0 ** -(exponent // 2), scale)
    for exponent in (64, 32, 16, 8, 4, 2, 1):
        small = peak * full * 2.0**exponent < 2.0
        full = jnp.where(small, full * 2.0**exponent, full)
        scale = jnp.where(small, scale * 2.0 ** (exponent // 2), scale)
    return scale if root else full


def inverse_factor(gram, work):
    rank = gram.shape[0]
    index = lax.broadcasted_iota(jnp.int32, (rank, 1), 0)
    lane = lax.broadcasted_iota(jnp.int32, (rank, 2 * rank), 1)
    work[:, :rank] = (lax.broadcasted_iota(jnp.int32, (rank, rank), 1) == index).astype(F32)
    work[:, rank:] = gram
    tiles = [work[at:at + 8, :] for at in range(0, rank, 8)]
    below = lax.broadcasted_iota(jnp.int32, (8, 1), 0)
    for k in range(rank - 1):
        at = rank + k
        first, inner = divmod(k, 8)
        row = tiles[first][inner:inner + 1, :]
        row = row * (1.0 / row[:, at:at + 1])
        for number in range(first, len(tiles)):
            column = tiles[number][:, at:at + 1]
            if number == first:
                column = jnp.where(below > inner, column, 0.0)
            tiles[number] = tiles[number] - column * row
    table = jnp.concatenate(tiles, axis=0)
    pivots = jnp.sum(jnp.where(lane == index + rank, table, 0.0), axis=1, keepdims=True)
    work[...] = table * lax.rsqrt(pivots)
    return work[:, :rank]


def slot_columns(place, gap, width):
    return pl.ds(pl.multiple_of((place ^ gap) * width, 128), width)


def add_products(place, gaps, pieces, delta, part):
    rows = delta.shape[0]
    block = min(256, rows)
    for start in range(0, rows, block):
        total = part[:, start:start + block]
        for gap, piece in zip(gaps, pieces):
            columns = slot_columns(place, gap, piece.shape[1])
            total += dot(piece[...], delta[start:start + block, columns], NT)
        part[:, start:start + block] = total


def part_kernel(gaps, fresh, place_ref, delta, *refs):
    pieces, refs = refs[:len(gaps)], refs[len(gaps):]
    out = refs[-1]
    out[...] = jnp.zeros_like(out) if fresh else refs[0][...]
    add_products(place_ref[0], gaps, pieces, delta, out)


def biggest(pieces):
    peak = None
    for piece in pieces:
        most = jnp.max(jnp.abs(piece[...]).astype(F32), keepdims=True)
        peak = most if peak is None else jnp.maximum(peak, most)
    return peak


def first_kernel(gaps, count, place_ref, delta, *refs):
    pieces, refs = refs[:count], refs[count:]
    before, out, part = refs
    part[...] = before[...]
    scale = power_scale(biggest(pieces)) * LIFT
    add_products(place_ref[0], gaps, [pieces[gap] for gap in gaps], delta, part)
    out[...] = (part[...] * scale).astype(BF16)


def second_kernel(gaps, count, place_ref, delta, *refs):
    pieces, refs = refs[:count], refs[count:]
    before, out, gram, part, work = refs
    part[...] = before[...]
    peak = biggest(pieces)
    scale = power_scale(peak)
    second = power_scale(peak * (1.0 / LIFT), root=True)
    right_gram = None
    for piece in pieces:
        scaled = (piece[...].astype(F32) * scale).astype(BF16)
        term = dot(scaled, scaled, NT)
        right_gram = term if right_gram is None else right_gram + term
    inverse = inverse_factor(right_gram, work) * second
    add_products(place_ref[0], gaps, [pieces[gap] for gap in gaps], delta, part)
    left = dot_wide(inverse, part[...] * scale).astype(BF16)
    out[...] = left
    gram[...] = dot(left, left, NT)


def delta_call(kernel, place, delta, args, out_shape, scratch, name):
    vmem = pl.BlockSpec(memory_space=pltpu.VMEM)
    return pl.pallas_call(
        kernel,
        in_specs=[pl.BlockSpec(memory_space=pltpu.SMEM)] + [vmem] * (1 + len(args)),
        out_specs=[vmem] * len(out_shape),
        out_shape=out_shape,
        scratch_shapes=scratch,
        compiler_params=pltpu.CompilerParams(vmem_limit_bytes=DELTA_VMEM_BYTES),
        name=name,
        cost_estimate=SHORT,
    )(place, pltpu.with_memory_space_constraint(delta, pltpu.VMEM), *args)


def left_sweep(kernel, place, delta, own, early, out_shape, scratch, name):
    rank, width = own.shape
    rows = delta.shape[0]
    count = lax.axis_size("rows")
    near = tuple(gap for gap in range(1, count) if not gap & (gap - 1))
    far = tuple(gap for gap in range(1, count) if gap & (gap - 1))

    def add(gaps, args):
        return delta_call(
            functools.partial(part_kernel, gaps, gaps[0] == 0), place, delta, args,
            [jax.ShapeDtypeStruct((rank, rows), F32)], [], name + "_part",
        )[0]

    arrived = [permute(own, "rows", gap) for gap in near]
    if early:
        part = add((0,), [own])
        part, *arrived = together(part, *arrived)
    pieces = [own] + [None] * (count - 1)
    for gap, piece in zip(near, arrived):
        pieces[gap] = piece
    forward(pieces, "rows")
    part = add(near, [*arrived, part]) if early else add((0, *near), [own, *arrived])
    return delta_call(
        functools.partial(kernel, far, count), place, delta, [*pieces, part], out_shape,
        [pltpu.VMEM((rank, rows), F32)] + scratch, name,
    )


def right_kernel_first(gap, place_ref, delta, left, out):
    width = out.shape[1]
    step = 1792 if width % 1792 == 0 else width
    for start in range(0, width, step):
        at = pl.ds(pl.multiple_of((place_ref[0] ^ gap) * width + start, 128), step)
        out[:, start:start + step] = dot(left[...], delta[:, at]).astype(BF16)


def right_kernel_second(gap, real, place_ref, delta, left, out):
    groups, _, size = out.shape
    slot = place_ref[0] ^ gap
    start = slot_start(slot, size, real)
    inside = lax.broadcasted_iota(jnp.int32, (1, size), 1) + start >= slot * size
    for group in range(groups):
        at = pl.ds(pl.multiple_of(group * real + start, 128), size)
        value = dot(left[...], delta[:, at])
        out[group] = jnp.where(inside, value, 0.0).astype(BF16)


def own_kernel_second(count, real, place_ref, delta, left, *refs):
    grams, (out, unit, inverse, work) = refs[:count], refs[count:]
    right_kernel_second(0, real, place_ref, delta, left, out)
    total = grams[0][...]
    for gram in grams[1:]:
        total = total + gram[...]
    factor = inverse_factor(total, work)
    inverse[...] = factor
    high_part, low_part = halves(factor)
    unit[...] = (dot(high_part, left[...]) + dot(low_part, left[...])).astype(BF16)


def slot_start(slot, size, real):
    return jnp.minimum(slot * size, real - size)


def small_call(kernel, out_shape, args, scratch=(), name=None, scalars=0):
    spec = lambda i: pl.BlockSpec(memory_space=pltpu.SMEM if i < scalars else pltpu.VMEM)
    return pl.pallas_call(
        kernel,
        in_specs=[spec(i) for i in range(len(args))],
        out_specs=[pl.BlockSpec(memory_space=pltpu.VMEM)] * len(out_shape),
        out_shape=out_shape,
        scratch_shapes=list(scratch),
        compiler_params=pltpu.CompilerParams(vmem_limit_bytes=VMEM_BYTES),
        name=name,
        cost_estimate=SHORT,
    )(*args)


def right_sum_kernel(count, *refs):
    parts, (total, gram) = refs[:count], refs[count:]
    result = None
    for group in range(total.shape[0]):
        value = parts[0][group].astype(F32)
        for part in parts[1:]:
            value = value + part[group].astype(F32)
        total[group] = value
        term = dot_wide(value, value, NT)
        result = term if result is None else result + term
    gram[...] = result


def right_kernel(count, groups, place_ref, weight_ref, total, left_inverse, *refs):
    grams, outs, (work,) = refs[:count], refs[count:count + groups], refs[count + groups:]
    gram = grams[0][...]
    for other in grams[1:]:
        gram = gram + other[...]
    factor = inverse_factor(gram, work)
    middle_high, middle_low = halves(weight_ref[0] * dot_wide(left_inverse[...], dot_wide(gram, factor, NT)))
    high, low = halves(factor)
    rank, size = total.shape[1:]
    for gap, out in enumerate(outs):
        value_high, value_low = halves(total[place_ref[0] ^ gap])
        out[:, :size] = (dot(high, value_high) + (dot(high, value_low) + dot(low, value_high))).astype(BF16)
        out[:, size:size + rank] = middle_high
        out[:, size + rank:] = middle_low


def grams_kernel(groups, place_ref, left_stack, *refs):
    pieces, (stack, middles, home, away, *slabs) = refs[:groups], refs[groups:]
    left_rows = slabs[0].shape[0]
    for gap, slab in enumerate(slabs):
        at = pl.multiple_of((place_ref[1] ^ gap) * left_rows, left_rows)
        slab[...] = dot(left_stack[pl.ds(at, left_rows), :], left_stack[...], NT).astype(BF16)
    rank = pieces[0].shape[0]
    size = stack.shape[1]
    place = place_ref[0]
    for gap, piece in enumerate(pieces):
        owner = place ^ gap
        stack[pl.ds(pl.multiple_of(owner * rank, rank), rank), :] = piece[:, :size]
        middles[owner] = piece[:, size:size + rank].astype(F32) + piece[:, size + rank:].astype(F32)
    for number in range(groups // 2):
        for out, gap in ((home, 2 * number), (away, 2 * number + 1)):
            at = pl.multiple_of((place ^ gap) * rank, rank)
            out[number] = dot(stack[pl.ds(at, rank), :], stack[...], NT).astype(BF16)


def fill_gram(place, pairs, gram):
    rank = pairs[0].shape[1]
    for number, pair in enumerate(pairs):
        for side in range(2):
            at = pl.multiple_of((place ^ (2 * number + side)) * rank, rank)
            gram[pl.ds(at, rank), :] = pair[side].astype(F32)


def polish(count, gram, product, spare, side):
    size = gram.shape[0]
    strip = min(512, size)
    eye = (
        lax.broadcasted_iota(jnp.int32, (size, size), 0) == lax.broadcasted_iota(jnp.int32, (size, size), 1)
    ).astype(F32)
    lead, tail = 1.5 / math.sqrt(count), -0.5 / (count * math.sqrt(count))
    product[...] = lead * eye + tail * gram[...]

    def multiply(a_ref, c_ref, lead, tail):
        def one(index, _):
            rows = pl.ds(pl.multiple_of(index * strip, strip), strip)
            a = a_ref[rows, :]
            c_ref[rows, :] = lead * a + tail * dot(a.astype(BF16), side[...])
            return 0

        lax.fori_loop(0, size // strip, one, 0)

    def step(index, _):
        first = index == 1
        before = jnp.where(first, lead, 1.5)
        after = jnp.where(first, tail, -0.5)
        side[...] = gram[...].astype(BF16)
        multiply(gram, spare, before, after)
        multiply(spare, gram, before, after)
        side[...] = gram[...].astype(BF16)
        multiply(product, product, 1.5, -0.5)
        return 0

    lax.fori_loop(1, NS_ITERS, step, 0)


def left_mix_kernel(count, ckpt_count, place_ref, *refs):
    slabs, (stack, middle, out, gram, product, spare, side) = refs[:count], refs[count:]
    slab_rows = slabs[0].shape[0]
    for gap, slab in enumerate(slabs):
        at = pl.multiple_of((place_ref[0] ^ gap) * slab_rows, slab_rows)
        gram[pl.ds(at, slab_rows), :] = slab[...].astype(F32)
    polish(ckpt_count, gram, product, spare, side)
    rank = middle.shape[1]
    for index in range(ckpt_count):
        rows = pl.ds(index * rank, rank)
        spare[rows, :] = dot_wide(jnp.transpose(middle[index]), product[rows, :])
    side[...] = spare[...].astype(BF16)
    out[...] = dot(side[...], stack[...]).astype(BF16)


def merge_kernel(count, ckpt_count, places_ref, mixed, *refs):
    pairs, refs = refs[:ckpt_count // 2], refs[ckpt_count // 2:]
    pieces, (out, gram, product, spare, side, wide) = refs[:count], refs[count:]
    real = out.shape[1]

    @pl.when(pl.program_id(0) == 0)
    def _():
        fill_gram(places_ref[0], pairs, gram)
        size = pieces[0].shape[1]
        wide[...] = jnp.zeros_like(wide)
        for gap, piece in enumerate(pieces):
            start = pl.multiple_of(slot_start(places_ref[1] ^ gap, size, real), 128)
            wide[:, pl.ds(start, size)] += piece[...]
        polish(ckpt_count, gram, product, spare, side)
        side[...] = product[...].astype(BF16)

    turned = jnp.transpose(dot(side[...], mixed[...])).astype(BF16)
    out[...] = dot(turned, wide[...]).astype(BF16)


def permute(value, axis, gap):
    count = lax.axis_size(axis)
    return lax.ppermute(value, axis, [(source, source ^ gap) for source in range(count)])


def spread(value, axis):
    return [value] + [permute(value, axis, gap) for gap in range(1, lax.axis_size(axis))]


def forward(got, axis):
    half = got[0].shape[0] // 2
    for gap in sorted(range(1, len(got)), key=lambda gap: bin(gap).count("1")):
        low, high = gap & -gap, 1 << (gap.bit_length() - 1)
        if low != high:
            got[gap] = jnp.concatenate([
                permute(got[gap ^ low][:half], axis, low), permute(got[gap ^ high][half:], axis, high)
            ])
    return got


def swap(values, axis):
    return [values[0]] + [permute(value, axis, gap) for gap, value in enumerate(values) if gap]


def right_sweep(call, left, count, small=()):
    parts = [None] * count
    for gap in range(count - 1, 0, -1):
        piece, left = together(call(gap, left), left)
        if small:
            left, *small = together(left, *small)
        parts[gap] = permute(piece, "rows", gap)
    if count > 2:
        left, parts[count - 1] = together(left, parts[count - 1])
    parts[0] = call(0, left, *small)
    return parts


def together(*values):
    return lax.optimization_barrier(values)


def add_up(values):
    return sum(value.astype(F32) for value in values)


def body(deltas, start_basis, edit_order):
    changes = deltas[0]
    start = jnp.transpose(start_basis[0])
    rank, width = start.shape
    rows, cols = changes.shape
    count = lax.axis_size("rows")
    groups = lax.axis_size("ckpt")
    row_place = lax.axis_index("rows").astype(jnp.int32)
    ckpt_place = lax.axis_index("ckpt").astype(jnp.int32)
    at_row = row_place[None]
    at_ckpt = ckpt_place[None]
    at_both = jnp.stack([ckpt_place, row_place])
    shape = jax.ShapeDtypeStruct
    square = shape((rank, rank), F32)
    work = pltpu.VMEM((rank, 2 * rank), F32)
    (left,) = left_sweep(
        first_kernel, at_row, changes, start, True, [shape((rank, rows), BF16)], [], "first_left"
    )
    parts = right_sweep(
        lambda gap, left: delta_call(
            functools.partial(right_kernel_first, gap), at_row, changes, [left], [shape((rank, width), BF16)], [],
            "first_right",
        )[0],
        left, count,
    )
    right = add_up(parts).astype(BF16)

    block = cols // groups
    padded = -(-block // (count * 128)) * 128
    left, left_gram = left_sweep(
        second_kernel, at_row, changes, right, True, [shape((rank, rows), BF16), square], [work], "second_left"
    )
    left_grams = spread(left_gram, "rows")

    def right_piece(gap, left, *grams):
        if gap:
            return delta_call(
                functools.partial(right_kernel_second, gap, block), at_row, changes, [left],
                [shape((groups, rank, padded), BF16)], [], "second_right",
            )[0]
        return delta_call(
            functools.partial(own_kernel_second, count, block), at_row, changes, [left, *grams],
            [shape((groups, rank, padded), BF16), shape((rank, rows), BF16), square], [work], "second_own",
        )

    parts = right_sweep(right_piece, left, count, left_grams)
    parts[0], left_unit, left_inverse = parts[0]
    left_unit, *arrived = together(left_unit, *parts[1:])
    parts[1:] = arrived
    left_stack = lax.all_gather(left_unit, "ckpt", axis=0, tiled=True)
    total, right_gram = small_call(
        functools.partial(right_sum_kernel, count), [shape((groups, rank, padded), F32), square], parts,
        name="right_sum",
    )
    position = jnp.sum(jnp.where(jnp.arange(groups) == ckpt_place, edit_order, 0))
    weight = (1 + position).astype(F32)[None] / groups
    leaving = small_call(
        functools.partial(right_kernel, count, groups), [shape((rank, padded + 2 * rank), BF16)] * groups,
        [at_ckpt, weight, total, left_inverse] + spread(right_gram, "rows"), [work], "right_unit", scalars=2,
    )
    pieces = swap(leaving, "ckpt")
    size = groups * rank
    table = pltpu.VMEM((size, size), F32)
    tables = [table, table, table, pltpu.VMEM((size, size), BF16)]
    slabs = shape((groups // 2, rank, size), BF16)
    right_stack, middles, home, away, *left_slabs = small_call(
        functools.partial(grams_kernel, groups),
        [shape((size, padded), BF16), shape((groups, rank, rank), F32), slabs, slabs]
        + [shape((size // count, size), BF16)] * count,
        [at_both, left_stack] + pieces, name="grams", scalars=1,
    )
    near = [permute(right_stack, "rows", gap) for gap in range(1, count) if not gap & (gap - 1)]
    pair_sum = add_up([home, permute(away, "ckpt", 1)]).astype(BF16)
    own = add_up([pair_sum[0]] + [permute(pair_sum[n], "ckpt", 2 * n) for n in range(1, groups // 2)]).astype(BF16)
    own, *held = together(own, *near, *left_slabs)
    near, left_slabs = held[:len(near)], held[len(near):]
    right_rows = add_up(spread(own, "rows")).astype(BF16)
    left_slab = add_up(swap(left_slabs, "rows")).astype(BF16)
    right_rows, left_slab = together(right_rows, left_slab)
    pair = jnp.stack([right_rows, permute(right_rows, "ckpt", 1)])
    pair, left_slab, *near = together(pair, left_slab, *near)
    right_pairs = [pair] + [permute(pair, "ckpt", gap) for gap in range(2, groups, 2)]
    left_slabs = spread(left_slab, "rows")
    right_all = [right_stack] + [None if gap & (gap - 1) else near.pop(0) for gap in range(1, count)]
    forward(right_all, "rows")

    (mixed,) = small_call(
        functools.partial(left_mix_kernel, count, groups), [shape((size, rows), BF16)],
        [at_row] + left_slabs + [left_stack, middles], tables, "left_mix", scalars=1,
    )
    step = min(512, rows)
    full = lambda value: pl.BlockSpec(value.shape, lambda i: (0,) * value.ndim)
    return pl.pallas_call(
        functools.partial(merge_kernel, count, groups),
        grid=(rows // step,),
        in_specs=[pl.BlockSpec(memory_space=pltpu.SMEM), pl.BlockSpec((size, step), lambda i: (0, i))]
        + [full(value) for value in right_pairs + right_all],
        out_specs=pl.BlockSpec((step, block), lambda i: (i, 0)),
        out_shape=shape((rows, block), BF16),
        scratch_shapes=tables + [pltpu.VMEM((size, block), BF16)],
        compiler_params=pltpu.CompilerParams(vmem_limit_bytes=VMEM_BYTES),
        name="merge",
        cost_estimate=SHORT,
    )(at_both, mixed, *right_pairs, *right_all)


def solution(mesh):
    return jax.shard_map(
        body,
        mesh=mesh,
        in_specs=(P("ckpt", "rows", None), P("ckpt", "rows", None), P()),
        out_specs=P("rows", "ckpt"),
        check_vma=False,
    )
```

```python
import functools
import math

import jax
import jax.numpy as jnp
from jax import lax
from jax.experimental import pallas as pl
from jax.experimental.pallas import tpu as pltpu
from jax.sharding import PartitionSpec as P

NS_ITERS = 4
LIFT = 2.0**60
VMEM_BYTES = 24 * 1024 * 1024
DELTA_VMEM_BYTES = 22 * 1024 * 1024
SHORT = pl.CostEstimate(flops=1024, bytes_accessed=1024, transcendentals=0)
F32 = jnp.float32
BF16 = jnp.bfloat16
NN = (((1,), (0,)), ((), ()))
NT = (((1,), (1,)), ((), ()))
TN = (((0,), (0,)), ((), ()))


def dot(a, b, dims=NN):
    return lax.dot_general(a, b, dims, preferred_element_type=F32)


def halves(x):
    high = x.astype(BF16)
    return high, (x - high.astype(F32)).astype(BF16)


def dot_wide(a, b, dims=NN):
    a_high, a_low = halves(a)
    b_high, b_low = halves(b)
    return dot(a_high, b_high, dims) + (dot(a_high, b_low, dims) + dot(a_low, b_high, dims))


def power_scale(peak, root=False):
    scale = jnp.ones_like(peak)
    full = jnp.ones_like(peak)
    for exponent in (64, 32, 16, 8, 4, 2, 1):
        big = peak * full >= 2.0**exponent
        full = jnp.where(big, full * 2.0**-exponent, full)
        scale = jnp.where(big, scale * 2.0 ** -(exponent // 2), scale)
    for exponent in (64, 32, 16, 8, 4, 2, 1):
        small = peak * full * 2.0**exponent < 2.0
        full = jnp.where(small, full * 2.0**exponent, full)
        scale = jnp.where(small, scale * 2.0 ** (exponent // 2), scale)
    return scale if root else full


def inverse_factor(gram, work):
    rank = gram.shape[0]
    index = lax.broadcasted_iota(jnp.int32, (rank, 1), 0)
    lane = lax.broadcasted_iota(jnp.int32, (rank, 2 * rank), 1)
    work[:, :rank] = (lax.broadcasted_iota(jnp.int32, (rank, rank), 1) == index).astype(F32)
    work[:, rank:] = gram
    tiles = [work[at:at + 8, :] for at in range(0, rank, 8)]
    below = lax.broadcasted_iota(jnp.int32, (8, 2 * rank), 0)
    for k in range(rank - 1):
        at = rank + k
        first, inner = divmod(k, 8)
        columns = [jnp.broadcast_to(tile[:, at:at + 1], tile.shape) for tile in tiles[first:]]
        row = tiles[first][inner:inner + 1, :] * (1.0 / columns[0][inner:inner + 1, :])
        columns[0] = jnp.where(below > inner, columns[0], 0.0)
        for number, column in enumerate(columns, first):
            tiles[number] = tiles[number] - column * row
    table = jnp.concatenate(tiles, axis=0)
    pivots = jnp.sum(jnp.where(lane == index + rank, table, 0.0), axis=1, keepdims=True)
    work[...] = table * lax.rsqrt(pivots)
    return work[:, :rank]


def slot_columns(place, gap, width):
    return pl.ds(pl.multiple_of((place ^ gap) * width, 128), width)


def add_products(place, gaps, pieces, delta, part):
    rows = delta.shape[0]
    block = min(256, rows)
    for start in range(0, rows, block):
        total = part[:, start:start + block]
        for gap, piece in zip(gaps, pieces):
            columns = slot_columns(place, gap, piece.shape[1])
            total += dot(piece[...], delta[start:start + block, columns], NT)
        part[:, start:start + block] = total


def part_kernel(gaps, fresh, place_ref, delta, *refs):
    pieces, refs = refs[:len(gaps)], refs[len(gaps):]
    out = refs[-1]
    out[...] = jnp.zeros_like(out) if fresh else refs[0][...]
    add_products(place_ref[0], gaps, pieces, delta, out)


def biggest(pieces):
    peak = None
    for piece in pieces:
        most = jnp.max(jnp.abs(piece[...]).astype(F32), keepdims=True)
        peak = most if peak is None else jnp.maximum(peak, most)
    return peak


def first_kernel(gaps, count, place_ref, delta, *refs):
    pieces, refs = refs[:count], refs[count:]
    before, out, part = refs
    part[...] = before[...]
    scale = power_scale(biggest(pieces)) * LIFT
    add_products(place_ref[0], gaps, [pieces[gap] for gap in gaps], delta, part)
    out[...] = (part[...] * scale).astype(BF16)


def second_kernel(gaps, count, place_ref, delta, *refs):
    pieces, refs = refs[:count], refs[count:]
    before, out, gram, part, work = refs
    part[...] = before[...]
    peak = biggest(pieces)
    scale = power_scale(peak)
    second = power_scale(peak * (1.0 / LIFT), root=True)
    right_gram = None
    for piece in pieces:
        scaled = (piece[...].astype(F32) * scale).astype(BF16)
        term = dot(scaled, scaled, NT)
        right_gram = term if right_gram is None else right_gram + term
    inverse = inverse_factor(right_gram, work) * second
    add_products(place_ref[0], gaps, [pieces[gap] for gap in gaps], delta, part)
    left = dot_wide(inverse, part[...] * scale).astype(BF16)
    out[...] = left
    gram[...] = dot(left, left, NT)


def delta_call(kernel, place, delta, args, out_shape, scratch, name):
    vmem = pl.BlockSpec(memory_space=pltpu.VMEM)
    return pl.pallas_call(
        kernel,
        in_specs=[pl.BlockSpec(memory_space=pltpu.SMEM)] + [vmem] * (1 + len(args)),
        out_specs=[vmem] * len(out_shape),
        out_shape=out_shape,
        scratch_shapes=scratch,
        compiler_params=pltpu.CompilerParams(vmem_limit_bytes=DELTA_VMEM_BYTES),
        name=name,
        cost_estimate=SHORT,
    )(place, pltpu.with_memory_space_constraint(delta, pltpu.VMEM), *args)


def left_sweep(kernel, place, delta, own, early, out_shape, scratch, name):
    rank, width = own.shape
    rows = delta.shape[0]
    count = lax.axis_size("rows")
    near = tuple(gap for gap in range(1, count) if not gap & (gap - 1))
    far = tuple(gap for gap in range(1, count) if gap & (gap - 1))

    def add(gaps, args):
        return delta_call(
            functools.partial(part_kernel, gaps, gaps[0] == 0), place, delta, args,
            [jax.ShapeDtypeStruct((rank, rows), F32)], [], name + "_part",
        )[0]

    arrived = [permute(own, "rows", gap) for gap in near]
    if early:
        part = add((0,), [own])
        part, *arrived = together(part, *arrived)
    pieces = [own] + [None] * (count - 1)
    for gap, piece in zip(near, arrived):
        pieces[gap] = piece
    forward(pieces, "rows")
    part = add(near, [*arrived, part]) if early else add((0, *near), [own, *arrived])
    return delta_call(
        functools.partial(kernel, far, count), place, delta, [*pieces, part], out_shape,
        [pltpu.VMEM((rank, rows), F32)] + scratch, name,
    )


def right_kernel_first(gap, place_ref, delta, left, out):
    width = out.shape[1]
    step = 1792 if width % 1792 == 0 else width
    for start in range(0, width, step):
        at = pl.ds(pl.multiple_of((place_ref[0] ^ gap) * width + start, 128), step)
        out[:, start:start + step] = dot(left[...], delta[:, at]).astype(BF16)


def right_kernel_second(gap, real, place_ref, delta, left, out):
    groups, _, size = out.shape
    slot = place_ref[0] ^ gap
    start = slot_start(slot, size, real)
    inside = lax.broadcasted_iota(jnp.int32, (1, size), 1) + start >= slot * size
    for group in range(groups):
        at = pl.ds(pl.multiple_of(group * real + start, 128), size)
        value = dot(left[...], delta[:, at])
        out[group] = jnp.where(inside, value, 0.0).astype(BF16)


def own_kernel_second(count, real, place_ref, delta, left, *refs):
    grams, (out, unit, inverse, work) = refs[:count], refs[count:]
    right_kernel_second(0, real, place_ref, delta, left, out)
    total = grams[0][...]
    for gram in grams[1:]:
        total = total + gram[...]
    factor = inverse_factor(total, work)
    inverse[...] = factor
    high_part, low_part = halves(factor)
    unit[...] = (dot(high_part, left[...]) + dot(low_part, left[...])).astype(BF16)


def slot_start(slot, size, real):
    return jnp.minimum(slot * size, real - size)


def small_call(kernel, out_shape, args, scratch=(), name=None, scalars=0):
    spec = lambda i: pl.BlockSpec(memory_space=pltpu.SMEM if i < scalars else pltpu.VMEM)
    return pl.pallas_call(
        kernel,
        in_specs=[spec(i) for i in range(len(args))],
        out_specs=[pl.BlockSpec(memory_space=pltpu.VMEM)] * len(out_shape),
        out_shape=out_shape,
        scratch_shapes=list(scratch),
        compiler_params=pltpu.CompilerParams(vmem_limit_bytes=VMEM_BYTES),
        name=name,
        cost_estimate=SHORT,
    )(*args)


def right_sum_kernel(count, *refs):
    parts, (total, gram) = refs[:count], refs[count:]
    result = None
    for group in range(total.shape[0]):
        value = parts[0][group].astype(F32)
        for part in parts[1:]:
            value = value + part[group].astype(F32)
        total[group] = value
        term = dot_wide(value, value, NT)
        result = term if result is None else result + term
    gram[...] = result


def right_kernel(count, groups, place_ref, weight_ref, total, left_inverse, *refs):
    grams, outs, (work,) = refs[:count], refs[count:count + groups], refs[count + groups:]
    gram = grams[0][...]
    for other in grams[1:]:
        gram = gram + other[...]
    factor = inverse_factor(gram, work)
    middle_high, middle_low = halves(weight_ref[0] * dot_wide(left_inverse[...], dot_wide(gram, factor, NT)))
    high, low = halves(factor)
    rank, size = total.shape[1:]
    for gap, out in enumerate(outs):
        value_high, value_low = halves(total[place_ref[0] ^ gap])
        out[:, :size] = (dot(high, value_high) + (dot(high, value_low) + dot(low, value_high))).astype(BF16)
        out[:, size:size + rank] = middle_high
        out[:, size + rank:] = middle_low


def grams_kernel(groups, place_ref, left_stack, *refs):
    pieces, (stack, middles, home, away, left_rows) = refs[:groups], refs[groups:]
    at = pl.multiple_of(place_ref[0] * left_rows.shape[0], left_rows.shape[0])
    left_rows[...] = dot(left_stack[pl.ds(at, left_rows.shape[0]), :], left_stack[...], NT).astype(BF16)
    rank = pieces[0].shape[0]
    size = stack.shape[1]
    place = place_ref[0]
    for gap, piece in enumerate(pieces):
        owner = place ^ gap
        stack[pl.ds(pl.multiple_of(owner * rank, rank), rank), :] = piece[:, :size]
        middles[owner] = piece[:, size:size + rank].astype(F32) + piece[:, size + rank:].astype(F32)
    for number in range(groups // 2):
        for out, gap in ((home, 2 * number), (away, 2 * number + 1)):
            at = pl.multiple_of((place ^ gap) * rank, rank)
            out[number] = dot(stack[pl.ds(at, rank), :], stack[...], NT).astype(BF16)


def polish(count, sides):
    size = sides[0][0].shape[0]
    eye = (
        lax.broadcasted_iota(jnp.int32, (size, size), 0) == lax.broadcasted_iota(jnp.int32, (size, size), 1)
    ).astype(F32)
    lead, tail = 1.5 / math.sqrt(count), -0.5 / (count * math.sqrt(count))
    strip = min(512, size)
    for gram, product, _, _ in sides:
        product[...] = lead * eye + tail * gram[...]

    def multiply(a_ref, c_ref, other, lead, tail):
        def one(index, _):
            rows = pl.ds(pl.multiple_of(index * strip, strip), strip)
            a = a_ref[rows, :]
            c_ref[rows, :] = lead * a + tail * dot(a.astype(BF16), other[...])
            return 0

        if strip == size:
            c_ref[...] = lead * a_ref[...] + tail * dot(a_ref[...].astype(BF16), other[...])
        else:
            lax.fori_loop(0, size // strip, one, 0)

    def step(index, _):
        first = index == 1
        before = jnp.where(first, lead, 1.5)
        after = jnp.where(first, tail, -0.5)
        for gram, _, _, other in sides:
            other[...] = gram[...].astype(BF16)
        for gram, _, spare, other in sides:
            multiply(gram, spare, other, before, after)
        for gram, _, spare, other in sides:
            multiply(spare, gram, other, before, after)
        for gram, _, _, other in sides:
            other[...] = gram[...].astype(BF16)
        for _, product, _, other in sides:
            multiply(product, product, other, 1.5, -0.5)
        return 0

    lax.fori_loop(1, NS_ITERS, step, 0)


def merge_kernel(count, ckpt_count, places_ref, stack, middle, *refs):
    columns, pieces, refs = refs[:2], refs[2:2 + count], refs[2 + count:]
    out, gram, product, spare, left_gram, left_product, left_spare, other, left_other, wide = refs
    real = out.shape[1]

    @pl.when(pl.program_id(0) == 0)
    def _():
        rank = middle.shape[1]
        for number in range(ckpt_count // 2):
            for side, column in enumerate(columns):
                rows = pl.ds(pl.multiple_of((places_ref[0] ^ (2 * number + side)) * rank, rank), rank)
                gram[rows, :] = column[number, :rank, :].astype(F32)
                left_gram[rows, :] = column[number, rank:, :].astype(F32)
        size = pieces[0].shape[1]
        wide[...] = jnp.zeros_like(wide)
        for gap, piece in enumerate(pieces):
            start = pl.multiple_of(slot_start(places_ref[1] ^ gap, size, real), 128)
            wide[:, pl.ds(start, size)] += piece[...]
        polish(ckpt_count, [(gram, product, spare, other), (left_gram, left_product, left_spare, left_other)])
        for index in range(ckpt_count):
            rows = pl.ds(index * rank, rank)
            left_spare[rows, :] = dot_wide(jnp.transpose(middle[index]), left_product[rows, :])
        other[...] = dot_wide(product[...], left_spare[...]).astype(BF16)

    turned = jnp.transpose(dot(other[...], stack[...])).astype(BF16)
    out[...] = dot(turned, wide[...]).astype(BF16)


def permute(value, axis, gap):
    count = lax.axis_size(axis)
    return lax.ppermute(value, axis, [(source, source ^ gap) for source in range(count)])


def spread(value, axis):
    return [value] + [permute(value, axis, gap) for gap in range(1, lax.axis_size(axis))]


def forward(got, axis):
    half = got[0].shape[0] // 2
    for gap in sorted(range(1, len(got)), key=lambda gap: bin(gap).count("1")):
        low, high = gap & -gap, 1 << (gap.bit_length() - 1)
        if low != high:
            got[gap] = jnp.concatenate([
                permute(got[gap ^ low][:half], axis, low), permute(got[gap ^ high][half:], axis, high)
            ])
    return got


def swap(values, axis):
    return [values[0]] + [permute(value, axis, gap) for gap, value in enumerate(values) if gap]


def right_sweep(call, left, count, small=()):
    parts = [None] * count
    for gap in range(count - 1, 0, -1):
        piece, left = together(call(gap, left), left)
        if small:
            left, *small = together(left, *small)
        parts[gap] = permute(piece, "rows", gap)
    if count > 2:
        left, parts[count - 1] = together(left, parts[count - 1])
    parts[0] = call(0, left, *small)
    return parts


def together(*values):
    return lax.optimization_barrier(values)


def add_up(values):
    return sum(value.astype(F32) for value in values)


def body(deltas, start_basis, edit_order):
    changes = deltas[0]
    start = jnp.transpose(start_basis[0])
    rank, width = start.shape
    rows, cols = changes.shape
    count = lax.axis_size("rows")
    groups = lax.axis_size("ckpt")
    row_place = lax.axis_index("rows").astype(jnp.int32)
    ckpt_place = lax.axis_index("ckpt").astype(jnp.int32)
    at_row = row_place[None]
    at_ckpt = ckpt_place[None]
    at_both = jnp.stack([ckpt_place, row_place])
    shape = jax.ShapeDtypeStruct
    square = shape((rank, rank), F32)
    work = pltpu.VMEM((rank, 2 * rank), F32)
    (left,) = left_sweep(
        first_kernel, at_row, changes, start, True, [shape((rank, rows), BF16)], [], "first_left"
    )
    parts = right_sweep(
        lambda gap, left: delta_call(
            functools.partial(right_kernel_first, gap), at_row, changes, [left], [shape((rank, width), BF16)], [],
            "first_right",
        )[0],
        left, count,
    )
    right = add_up(parts).astype(BF16)

    block = cols // groups
    padded = -(-block // (count * 128)) * 128
    left, left_gram = left_sweep(
        second_kernel, at_row, changes, right, True, [shape((rank, rows), BF16), square], [work], "second_left"
    )
    left_grams = spread(left_gram, "rows")

    def right_piece(gap, left, *grams):
        if gap:
            return delta_call(
                functools.partial(right_kernel_second, gap, block), at_row, changes, [left],
                [shape((groups, rank, padded), BF16)], [], "second_right",
            )[0]
        return delta_call(
            functools.partial(own_kernel_second, count, block), at_row, changes, [left, *grams],
            [shape((groups, rank, padded), BF16), shape((rank, rows), BF16), square], [work], "second_own",
        )

    parts = right_sweep(right_piece, left, count, left_grams)
    parts[0], left_unit, left_inverse = parts[0]
    left_unit, *arrived = together(left_unit, *parts[1:])
    parts[1:] = arrived
    left_stack = lax.all_gather(left_unit, "ckpt", axis=0, tiled=True)
    total, right_gram = small_call(
        functools.partial(right_sum_kernel, count), [shape((groups, rank, padded), F32), square], parts,
        name="right_sum",
    )
    position = jnp.sum(jnp.where(jnp.arange(groups) == ckpt_place, edit_order, 0))
    weight = (1 + position).astype(F32)[None] / groups
    leaving = small_call(
        functools.partial(right_kernel, count, groups), [shape((rank, padded + 2 * rank), BF16)] * groups,
        [at_ckpt, weight, total, left_inverse] + spread(right_gram, "rows"), [work], "right_unit", scalars=2,
    )
    pieces = swap(leaving, "ckpt")
    size = groups * rank
    slabs = shape((groups // 2, rank, size), BF16)
    right_stack, middles, home, away, left_rows = small_call(
        functools.partial(grams_kernel, groups),
        [shape((size, padded), BF16), shape((groups, rank, rank), F32), slabs, slabs, shape((rank, size), BF16)],
        [at_ckpt, left_stack] + pieces, name="grams", scalars=1,
    )
    pair_sum = add_up([home, permute(away, "ckpt", 1)]).astype(BF16)
    right_stack, pair_sum = together(right_stack, pair_sum)
    own = add_up([pair_sum[0]] + [permute(pair_sum[n], "ckpt", 2 * n) for n in range(1, groups // 2)]).astype(BF16)
    near = [permute(right_stack, "rows", gap) for gap in range(1, count) if not gap & (gap - 1)]
    both = add_up(spread(jnp.concatenate([own, left_rows]), "rows")).astype(BF16)
    both, *near = together(both, *near)
    right_all = [right_stack] + [None if gap & (gap - 1) else near.pop(0) for gap in range(1, count)]
    forward(right_all, "rows")
    column = jnp.stack([both] + [permute(both, "ckpt", gap) for gap in range(2, groups, 2)])
    column, *right_all = together(column, *right_all)
    columns = [column, permute(column, "ckpt", 1)]

    step = min(512, rows)
    full = lambda value: pl.BlockSpec(value.shape, lambda i: (0,) * value.ndim)
    return pl.pallas_call(
        functools.partial(merge_kernel, count, groups),
        grid=(rows // step,),
        in_specs=[pl.BlockSpec(memory_space=pltpu.SMEM), pl.BlockSpec((size, step), lambda i: (0, i))]
        + [full(value) for value in [middles] + columns + right_all],
        out_specs=pl.BlockSpec((step, block), lambda i: (i, 0)),
        out_shape=shape((rows, block), BF16),
        scratch_shapes=[pltpu.VMEM((size, size), F32)] * 6 + [pltpu.VMEM((size, size), BF16)] * 2
        + [pltpu.VMEM((size, block), BF16)],
        compiler_params=pltpu.CompilerParams(vmem_limit_bytes=2 * VMEM_BYTES),
        name="merge",
        cost_estimate=SHORT,
    )(at_both, left_stack, middles, *columns, *right_all)


def solution(mesh):
    return jax.shard_map(
        body,
        mesh=mesh,
        in_specs=(P("ckpt", "rows", None), P("ckpt", "rows", None), P()),
        out_specs=P("rows", "ckpt"),
        check_vma=False,
    )
```

```python
import functools
import math

import jax
import jax.numpy as jnp
from jax import lax
from jax.experimental import pallas as pl
from jax.experimental.pallas import tpu as pltpu
from jax.sharding import PartitionSpec as P

NS_ITERS = 4
LIFT = 2.0**60
VMEM_BYTES = 24 * 1024 * 1024
DELTA_VMEM_BYTES = 22 * 1024 * 1024
SHORT = pl.CostEstimate(flops=1024, bytes_accessed=1024, transcendentals=0)
F32 = jnp.float32
BF16 = jnp.bfloat16
NN = (((1,), (0,)), ((), ()))
NT = (((1,), (1,)), ((), ()))
TN = (((0,), (0,)), ((), ()))


def dot(a, b, dims=NN):
    return lax.dot_general(a, b, dims, preferred_element_type=F32)


def halves(x):
    high = x.astype(BF16)
    return high, (x - high.astype(F32)).astype(BF16)


def dot_wide(a, b, dims=NN):
    a_high, a_low = halves(a)
    b_high, b_low = halves(b)
    return dot(a_high, b_high, dims) + (dot(a_high, b_low, dims) + dot(a_low, b_high, dims))


def power_scale(peak, root=False):
    scale = jnp.ones_like(peak)
    full = jnp.ones_like(peak)
    for exponent in (64, 32, 16, 8, 4, 2, 1):
        big = peak * full >= 2.0**exponent
        full = jnp.where(big, full * 2.0**-exponent, full)
        scale = jnp.where(big, scale * 2.0 ** -(exponent // 2), scale)
    for exponent in (64, 32, 16, 8, 4, 2, 1):
        small = peak * full * 2.0**exponent < 2.0
        full = jnp.where(small, full * 2.0**exponent, full)
        scale = jnp.where(small, scale * 2.0 ** (exponent // 2), scale)
    return scale if root else full


def inverse_factor(gram, work):
    rank = gram.shape[0]
    index = lax.broadcasted_iota(jnp.int32, (rank, 1), 0)
    lane = lax.broadcasted_iota(jnp.int32, (rank, 2 * rank), 1)
    work[:, :rank] = (lax.broadcasted_iota(jnp.int32, (rank, rank), 1) == index).astype(F32)
    work[:, rank:] = gram
    tiles = [work[at:at + 8, :] for at in range(0, rank, 8)]
    below = lax.broadcasted_iota(jnp.int32, (8, 2 * rank), 0)
    for k in range(rank - 1):
        at = rank + k
        first, inner = divmod(k, 8)
        columns = [jnp.broadcast_to(tile[:, at:at + 1], tile.shape) for tile in tiles[first:]]
        row = tiles[first][inner:inner + 1, :] * (1.0 / columns[0][inner:inner + 1, :])
        columns[0] = jnp.where(below > inner, columns[0], 0.0)
        for number, column in enumerate(columns, first):
            tiles[number] = tiles[number] - column * row
    table = jnp.concatenate(tiles, axis=0)
    pivots = jnp.sum(jnp.where(lane == index + rank, table, 0.0), axis=1, keepdims=True)
    work[...] = table * lax.rsqrt(pivots)
    return work[:, :rank]


def slot_columns(place, gap, width):
    return pl.ds(pl.multiple_of((place ^ gap) * width, 128), width)


def add_products(place, gaps, pieces, delta, part):
    rows = delta.shape[0]
    block = min(256, rows)
    for start in range(0, rows, block):
        total = part[:, start:start + block]
        for gap, piece in zip(gaps, pieces):
            columns = slot_columns(place, gap, piece.shape[1])
            total += dot(piece[...], delta[start:start + block, columns], NT)
        part[:, start:start + block] = total


def part_kernel(gaps, fresh, place_ref, delta, *refs):
    pieces, refs = refs[:len(gaps)], refs[len(gaps):]
    out = refs[-1]
    out[...] = jnp.zeros_like(out) if fresh else refs[0][...]
    add_products(place_ref[0], gaps, pieces, delta, out)


def biggest(pieces):
    peak = None
    for piece in pieces:
        most = jnp.max(jnp.abs(piece[...]).astype(F32), keepdims=True)
        peak = most if peak is None else jnp.maximum(peak, most)
    return peak


def first_kernel(gaps, count, place_ref, delta, *refs):
    pieces, refs = refs[:count], refs[count:]
    before, out, part = refs
    part[...] = before[...]
    scale = power_scale(biggest(pieces)) * LIFT
    add_products(place_ref[0], gaps, [pieces[gap] for gap in gaps], delta, part)
    out[...] = (part[...] * scale).astype(BF16)


def second_kernel(gaps, count, place_ref, delta, *refs):
    pieces, refs = refs[:count], refs[count:]
    before, out, gram, part, work = refs
    part[...] = before[...]
    peak = biggest(pieces)
    scale = power_scale(peak)
    second = power_scale(peak * (1.0 / LIFT), root=True)
    right_gram = None
    for piece in pieces:
        scaled = (piece[...].astype(F32) * scale).astype(BF16)
        term = dot(scaled, scaled, NT)
        right_gram = term if right_gram is None else right_gram + term
    inverse = inverse_factor(right_gram, work) * second
    add_products(place_ref[0], gaps, [pieces[gap] for gap in gaps], delta, part)
    left = dot_wide(inverse, part[...] * scale).astype(BF16)
    out[...] = left
    gram[...] = dot(left, left, NT)


def delta_call(kernel, place, delta, args, out_shape, scratch, name):
    vmem = pl.BlockSpec(memory_space=pltpu.VMEM)
    return pl.pallas_call(
        kernel,
        in_specs=[pl.BlockSpec(memory_space=pltpu.SMEM)] + [vmem] * (1 + len(args)),
        out_specs=[vmem] * len(out_shape),
        out_shape=out_shape,
        scratch_shapes=scratch,
        compiler_params=pltpu.CompilerParams(vmem_limit_bytes=DELTA_VMEM_BYTES),
        name=name,
        cost_estimate=SHORT,
    )(place, pltpu.with_memory_space_constraint(delta, pltpu.VMEM), *args)


def left_sweep(kernel, place, delta, own, early, out_shape, scratch, name):
    rank, width = own.shape
    rows = delta.shape[0]
    count = lax.axis_size("rows")
    near = tuple(gap for gap in range(1, count) if not gap & (gap - 1))
    far = tuple(gap for gap in range(1, count) if gap & (gap - 1))

    def add(gaps, args):
        return delta_call(
            functools.partial(part_kernel, gaps, gaps[0] == 0), place, delta, args,
            [jax.ShapeDtypeStruct((rank, rows), F32)], [], name + "_part",
        )[0]

    arrived = [permute(own, "rows", gap) for gap in near]
    if early:
        part = add((0,), [own])
        part, *arrived = together(part, *arrived)
    pieces = [own] + [None] * (count - 1)
    for gap, piece in zip(near, arrived):
        pieces[gap] = piece
    forward(pieces, "rows")
    part = add(near, [*arrived, part]) if early else add((0, *near), [own, *arrived])
    return delta_call(
        functools.partial(kernel, far, count), place, delta, [*pieces, part], out_shape,
        [pltpu.VMEM((rank, rows), F32)] + scratch, name,
    )


def right_kernel_first(gap, place_ref, delta, left, out):
    width = out.shape[1]
    step = 1792 if width % 1792 == 0 else width
    for start in range(0, width, step):
        at = pl.ds(pl.multiple_of((place_ref[0] ^ gap) * width + start, 128), step)
        out[:, start:start + step] = dot(left[...], delta[:, at]).astype(BF16)


def right_kernel_second(gap, real, place_ref, delta, left, out):
    groups, _, size = out.shape
    slot = place_ref[0] ^ gap
    start = slot_start(slot, size, real)
    inside = lax.broadcasted_iota(jnp.int32, (1, size), 1) + start >= slot * size
    for group in range(groups):
        at = pl.ds(pl.multiple_of(group * real + start, 128), size)
        value = dot(left[...], delta[:, at])
        out[group] = jnp.where(inside, value, 0.0).astype(BF16)


def own_kernel_second(count, real, place_ref, delta, left, *refs):
    grams, (out, unit, inverse, work) = refs[:count], refs[count:]
    right_kernel_second(0, real, place_ref, delta, left, out)
    total = grams[0][...]
    for gram in grams[1:]:
        total = total + gram[...]
    factor = inverse_factor(total, work)
    inverse[...] = factor
    high_part, low_part = halves(factor)
    unit[...] = (dot(high_part, left[...]) + dot(low_part, left[...])).astype(BF16)


def slot_start(slot, size, real):
    return jnp.minimum(slot * size, real - size)


def small_call(kernel, out_shape, args, scratch=(), name=None, scalars=0, hbm=0):
    spaces = [pltpu.SMEM] * scalars + [pltpu.HBM] * hbm + [pltpu.VMEM] * (len(args) - scalars - hbm)
    spec = lambda i: pl.BlockSpec(memory_space=spaces[i])
    return pl.pallas_call(
        kernel,
        in_specs=[spec(i) for i in range(len(args))],
        out_specs=[pl.BlockSpec(memory_space=pltpu.VMEM)] * len(out_shape),
        out_shape=out_shape,
        scratch_shapes=list(scratch),
        compiler_params=pltpu.CompilerParams(vmem_limit_bytes=VMEM_BYTES),
        name=name,
        cost_estimate=SHORT,
    )(*args)


def right_sum_kernel(count, *refs):
    parts, (total, gram) = refs[:count], refs[count:]
    result = None
    for group in range(total.shape[0]):
        value = parts[0][group].astype(F32)
        for part in parts[1:]:
            value = value + part[group].astype(F32)
        total[group] = value
        term = dot_wide(value, value, NT)
        result = term if result is None else result + term
    gram[...] = result


def right_kernel(count, groups, place_ref, weight_ref, total, left_inverse, *refs):
    grams, outs, (work,) = refs[:count], refs[count:count + groups], refs[count + groups:]
    gram = grams[0][...]
    for other in grams[1:]:
        gram = gram + other[...]
    factor = inverse_factor(gram, work)
    middle_high, middle_low = halves(weight_ref[0] * dot_wide(left_inverse[...], dot_wide(gram, factor, NT)))
    high, low = halves(factor)
    rank, size = total.shape[1:]
    for gap, out in enumerate(outs):
        value_high, value_low = halves(total[place_ref[0] ^ gap])
        out[:, :size] = (dot(high, value_high) + (dot(high, value_low) + dot(low, value_high))).astype(BF16)
        out[:, size:size + rank] = middle_high
        out[:, size + rank:] = middle_low


def grams_kernel(groups, place_ref, left_hbm, *refs):
    pieces, (stack, middles, home, away, left_rows, left_stack, sem) = refs[:groups], refs[groups:]
    copy = pltpu.make_async_copy(left_hbm, left_stack, sem)
    copy.start()
    rank = pieces[0].shape[0]
    size = stack.shape[1]
    place = place_ref[0]
    for gap, piece in enumerate(pieces):
        owner = place ^ gap
        stack[pl.ds(pl.multiple_of(owner * rank, rank), rank), :] = piece[:, :size]
        middles[owner] = piece[:, size:size + rank].astype(F32) + piece[:, size + rank:].astype(F32)
    for number in range(groups // 2):
        for out, gap in ((home, 2 * number), (away, 2 * number + 1)):
            at = pl.multiple_of((place ^ gap) * rank, rank)
            out[number] = dot(stack[pl.ds(at, rank), :], stack[...], NT).astype(BF16)
    copy.wait()
    at = pl.multiple_of(place * rank, rank)
    left_rows[...] = dot(left_stack[pl.ds(at, rank), :], left_stack[...], NT).astype(BF16)


def polish(count, sides):
    size = sides[0][0].shape[0]
    eye = (
        lax.broadcasted_iota(jnp.int32, (size, size), 0) == lax.broadcasted_iota(jnp.int32, (size, size), 1)
    ).astype(F32)
    lead, tail = 1.5 / math.sqrt(count), -0.5 / (count * math.sqrt(count))
    strip = min(512, size)
    for gram, product, _, _ in sides:
        product[...] = lead * eye + tail * gram[...]

    def multiply(a_ref, c_ref, other, lead, tail):
        def one(index, _):
            rows = pl.ds(pl.multiple_of(index * strip, strip), strip)
            a = a_ref[rows, :]
            c_ref[rows, :] = lead * a + tail * dot(a.astype(BF16), other[...])
            return 0

        if strip == size:
            c_ref[...] = lead * a_ref[...] + tail * dot(a_ref[...].astype(BF16), other[...])
        else:
            lax.fori_loop(0, size // strip, one, 0)

    def step(index, _):
        first = index == 1
        before = jnp.where(first, lead, 1.5)
        after = jnp.where(first, tail, -0.5)
        for gram, _, _, other in sides:
            other[...] = gram[...].astype(BF16)
        for gram, _, spare, other in sides:
            multiply(gram, spare, other, before, after)
        for gram, _, spare, other in sides:
            multiply(spare, gram, other, before, after)
        for gram, _, _, other in sides:
            other[...] = gram[...].astype(BF16)
        for _, product, _, other in sides:
            multiply(product, product, other, 1.5, -0.5)
        return 0

    lax.fori_loop(1, NS_ITERS, step, 0)


def merge_kernel(count, ckpt_count, places_ref, left_hbm, middle, *refs):
    columns, pieces, refs = refs[:2], refs[2:2 + count], refs[2 + count:]
    out, gram, product, spare, left_gram, left_product, left_spare, other, left_other, wide, strips, stack, sem, sems = refs
    real = out.shape[1]
    load = pltpu.make_async_copy(left_hbm, stack, sem)
    load.start()
    rank = middle.shape[1]
    for number in range(ckpt_count // 2):
        for side, column in enumerate(columns):
            rows = pl.ds(pl.multiple_of((places_ref[0] ^ (2 * number + side)) * rank, rank), rank)
            gram[rows, :] = column[number, :rank, :].astype(F32)
            left_gram[rows, :] = column[number, rank:, :].astype(F32)
    size = pieces[0].shape[1]
    wide[...] = jnp.zeros_like(wide)
    for gap, piece in enumerate(pieces):
        start = pl.multiple_of(slot_start(places_ref[1] ^ gap, size, real), 128)
        wide[:, pl.ds(start, size)] += piece[...]
    polish(ckpt_count, [(gram, product, spare, other), (left_gram, left_product, left_spare, left_other)])
    for index in range(ckpt_count):
        rows = pl.ds(index * rank, rank)
        left_spare[rows, :] = dot_wide(jnp.transpose(middle[index]), left_product[rows, :])
    other[...] = dot_wide(product[...], left_spare[...]).astype(BF16)

    load.wait()
    copies = []
    for number in range(strips.shape[0]):
        span = slice(number * strips.shape[1], (number + 1) * strips.shape[1])
        turned = jnp.transpose(dot(other[...], stack[:, span])).astype(BF16)
        strips[number] = dot(turned, wide[...]).astype(BF16)
        copy = pltpu.make_async_copy(strips.at[number], out.at[pl.ds(span.start, strips.shape[1]), :], sems.at[number])
        copy.start()
        copies.append(copy)
    for copy in copies:
        copy.wait()


def permute(value, axis, gap):
    count = lax.axis_size(axis)
    return lax.ppermute(value, axis, [(source, source ^ gap) for source in range(count)])


def spread(value, axis):
    return [value] + [permute(value, axis, gap) for gap in range(1, lax.axis_size(axis))]


def forward(got, axis):
    half = got[0].shape[0] // 2
    for gap in sorted(range(1, len(got)), key=lambda gap: bin(gap).count("1")):
        low, high = gap & -gap, 1 << (gap.bit_length() - 1)
        if low != high:
            got[gap] = jnp.concatenate([
                permute(got[gap ^ low][:half], axis, low), permute(got[gap ^ high][half:], axis, high)
            ])
    return got


def swap(values, axis):
    return [values[0]] + [permute(value, axis, gap) for gap, value in enumerate(values) if gap]


def right_sweep(call, left, count, small=()):
    parts = [None] * count
    for gap in range(count - 1, 0, -1):
        piece, left = together(call(gap, left), left)
        if small:
            left, *small = together(left, *small)
        parts[gap] = permute(piece, "rows", gap)
    if count > 2:
        left, parts[count - 1] = together(left, parts[count - 1])
    parts[0] = call(0, left, *small)
    return parts


def together(*values):
    return lax.optimization_barrier(values)


def add_up(values):
    return sum(value.astype(F32) for value in values)


def body(deltas, start_basis, edit_order):
    changes = deltas[0]
    start = jnp.transpose(start_basis[0])
    rank, width = start.shape
    rows, cols = changes.shape
    count = lax.axis_size("rows")
    groups = lax.axis_size("ckpt")
    row_place = lax.axis_index("rows").astype(jnp.int32)
    ckpt_place = lax.axis_index("ckpt").astype(jnp.int32)
    at_row = row_place[None]
    at_ckpt = ckpt_place[None]
    at_both = jnp.stack([ckpt_place, row_place])
    shape = jax.ShapeDtypeStruct
    square = shape((rank, rank), F32)
    work = pltpu.VMEM((rank, 2 * rank), F32)
    (left,) = left_sweep(
        first_kernel, at_row, changes, start, True, [shape((rank, rows), BF16)], [], "first_left"
    )
    parts = right_sweep(
        lambda gap, left: delta_call(
            functools.partial(right_kernel_first, gap), at_row, changes, [left], [shape((rank, width), BF16)], [],
            "first_right",
        )[0],
        left, count,
    )
    right = add_up(parts).astype(BF16)

    block = cols // groups
    padded = -(-block // (count * 128)) * 128
    left, left_gram = left_sweep(
        second_kernel, at_row, changes, right, True, [shape((rank, rows), BF16), square], [work], "second_left"
    )
    left_grams = spread(left_gram, "rows")

    def right_piece(gap, left, *grams):
        if gap:
            return delta_call(
                functools.partial(right_kernel_second, gap, block), at_row, changes, [left],
                [shape((groups, rank, padded), BF16)], [], "second_right",
            )[0]
        return delta_call(
            functools.partial(own_kernel_second, count, block), at_row, changes, [left, *grams],
            [shape((groups, rank, padded), BF16), shape((rank, rows), BF16), square], [work], "second_own",
        )

    parts = right_sweep(right_piece, left, count, left_grams)
    parts[0], left_unit, left_inverse = parts[0]
    left_unit, *arrived = together(left_unit, *parts[1:])
    parts[1:] = arrived
    left_stack = lax.all_gather(left_unit, "ckpt", axis=0, tiled=True)
    total, right_gram = small_call(
        functools.partial(right_sum_kernel, count), [shape((groups, rank, padded), F32), square], parts,
        name="right_sum",
    )
    position = jnp.sum(jnp.where(jnp.arange(groups) == ckpt_place, edit_order, 0))
    weight = (1 + position).astype(F32)[None] / groups
    leaving = small_call(
        functools.partial(right_kernel, count, groups), [shape((rank, padded + 2 * rank), BF16)] * groups,
        [at_ckpt, weight, total, left_inverse] + spread(right_gram, "rows"), [work], "right_unit", scalars=2,
    )
    pieces = swap(leaving, "ckpt")
    size = groups * rank
    slabs = shape((groups // 2, rank, size), BF16)
    in_hbm = pltpu.with_memory_space_constraint(left_stack, pltpu.HBM)
    right_stack, middles, home, away, left_rows = small_call(
        functools.partial(grams_kernel, groups),
        [shape((size, padded), BF16), shape((groups, rank, rank), F32), slabs, slabs, shape((rank, size), BF16)],
        [at_ckpt, in_hbm] + pieces, [pltpu.VMEM(left_stack.shape, BF16), pltpu.SemaphoreType.DMA(())],
        name="grams", scalars=1, hbm=1,
    )
    pair_sum = add_up([home, permute(away, "ckpt", 1)]).astype(BF16)
    right_stack, pair_sum = together(right_stack, pair_sum)
    own = add_up([pair_sum[0]] + [permute(pair_sum[n], "ckpt", 2 * n) for n in range(1, groups // 2)]).astype(BF16)
    near = [permute(right_stack, "rows", gap) for gap in range(1, count) if not gap & (gap - 1)]
    both = add_up(spread(jnp.concatenate([own, left_rows]), "rows")).astype(BF16)
    both, *near = together(both, *near)
    right_all = [right_stack] + [None if gap & (gap - 1) else near.pop(0) for gap in range(1, count)]
    forward(right_all, "rows")
    column = jnp.stack([both] + [permute(both, "ckpt", gap) for gap in range(2, groups, 2)])
    column, *right_all = together(column, *right_all)
    columns = [column, permute(column, "ckpt", 1)]

    step = min(256, rows)
    vmem = pl.BlockSpec(memory_space=pltpu.VMEM)
    args = [in_hbm, middles, *columns, *right_all]
    return pl.pallas_call(
        functools.partial(merge_kernel, count, groups),
        in_specs=[pl.BlockSpec(memory_space=pltpu.SMEM), pl.BlockSpec(memory_space=pltpu.HBM)] + [vmem] * (len(args) - 1),
        out_specs=pl.BlockSpec(memory_space=pl.ANY),
        out_shape=shape((rows, block), BF16),
        scratch_shapes=[pltpu.VMEM((size, size), F32)] * 6 + [pltpu.VMEM((size, size), BF16)] * 2
        + [pltpu.VMEM((size, block), BF16), pltpu.VMEM((rows // step, step, block), BF16),
           pltpu.VMEM(left_stack.shape, BF16), pltpu.SemaphoreType.DMA(()), pltpu.SemaphoreType.DMA((rows // step,))],
        compiler_params=pltpu.CompilerParams(vmem_limit_bytes=2 * VMEM_BYTES),
        name="merge",
        cost_estimate=SHORT,
    )(at_both, *args)


def solution(mesh):
    return jax.shard_map(
        body,
        mesh=mesh,
        in_specs=(P("ckpt", "rows", None), P("ckpt", "rows", None), P()),
        out_specs=P("rows", "ckpt"),
        check_vma=False,
    )
```

```python
import functools
import math

import jax
import jax.numpy as jnp
from jax import lax
from jax.experimental import pallas as pl
from jax.experimental.pallas import tpu as pltpu
from jax.sharding import PartitionSpec as P

NS_ITERS = 4
LIFT = 2.0**60
VMEM_BYTES = 24 * 1024 * 1024
DELTA_VMEM_BYTES = 22 * 1024 * 1024
SHORT = pl.CostEstimate(flops=1024, bytes_accessed=1024, transcendentals=0)
F32 = jnp.float32
BF16 = jnp.bfloat16
NN = (((1,), (0,)), ((), ()))
NT = (((1,), (1,)), ((), ()))
TN = (((0,), (0,)), ((), ()))


def dot(a, b, dims=NN):
    return lax.dot_general(a, b, dims, preferred_element_type=F32)


def halves(x):
    high = x.astype(BF16)
    return high, (x - high.astype(F32)).astype(BF16)


def dot_wide(a, b, dims=NN):
    a_high, a_low = halves(a)
    b_high, b_low = halves(b)
    return dot(a_high, b_high, dims) + (dot(a_high, b_low, dims) + dot(a_low, b_high, dims))


def power_scale(peak, root=False):
    scale = jnp.ones_like(peak)
    full = jnp.ones_like(peak)
    for exponent in (64, 32, 16, 8, 4, 2, 1):
        big = peak * full >= 2.0**exponent
        full = jnp.where(big, full * 2.0**-exponent, full)
        scale = jnp.where(big, scale * 2.0 ** -(exponent // 2), scale)
    for exponent in (64, 32, 16, 8, 4, 2, 1):
        small = peak * full * 2.0**exponent < 2.0
        full = jnp.where(small, full * 2.0**exponent, full)
        scale = jnp.where(small, scale * 2.0 ** (exponent // 2), scale)
    return scale if root else full


def inverse_factor(gram, work):
    rank = gram.shape[0]
    index = lax.broadcasted_iota(jnp.int32, (rank, 1), 0)
    lane = lax.broadcasted_iota(jnp.int32, (rank, 2 * rank), 1)
    work[:, :rank] = (lax.broadcasted_iota(jnp.int32, (rank, rank), 1) == index).astype(F32)
    work[:, rank:] = gram
    tiles = [work[at:at + 8, :] for at in range(0, rank, 8)]
    below = lax.broadcasted_iota(jnp.int32, (8, 2 * rank), 0)
    for k in range(rank - 1):
        at = rank + k
        first, inner = divmod(k, 8)
        columns = [jnp.broadcast_to(tile[:, at:at + 1], tile.shape) for tile in tiles[first:]]
        row = tiles[first][inner:inner + 1, :] * (1.0 / columns[0][inner:inner + 1, :])
        columns[0] = jnp.where(below > inner, columns[0], 0.0)
        for number, column in enumerate(columns, first):
            tiles[number] = tiles[number] - column * row
    table = jnp.concatenate(tiles, axis=0)
    pivots = jnp.sum(jnp.where(lane == index + rank, table, 0.0), axis=1, keepdims=True)
    work[...] = table * lax.rsqrt(pivots)
    return work[:, :rank]


def slot_columns(place, gap, width):
    return pl.ds(pl.multiple_of((place ^ gap) * width, 128), width)


def add_products(place, gaps, pieces, delta, part):
    rows = delta.shape[0]
    block = min(256, rows)
    for start in range(0, rows, block):
        total = part[:, start:start + block]
        for gap, piece in zip(gaps, pieces):
            columns = slot_columns(place, gap, piece.shape[1])
            total += dot(piece[...], delta[start:start + block, columns], NT)
        part[:, start:start + block] = total


def part_kernel(gaps, fresh, place_ref, delta, *refs):
    pieces, refs = refs[:len(gaps)], refs[len(gaps):]
    out = refs[-1]
    out[...] = jnp.zeros_like(out) if fresh else refs[0][...]
    add_products(place_ref[0], gaps, pieces, delta, out)


def biggest(pieces):
    peak = None
    for piece in pieces:
        most = jnp.max(jnp.abs(piece[...]).astype(F32), keepdims=True)
        peak = most if peak is None else jnp.maximum(peak, most)
    return peak


def first_kernel(gaps, count, place_ref, delta, *refs):
    pieces, refs = refs[:count], refs[count:]
    before, out, part = refs
    part[...] = before[...]
    scale = power_scale(biggest(pieces)) * LIFT
    add_products(place_ref[0], gaps, [pieces[gap] for gap in gaps], delta, part)
    out[...] = (part[...] * scale).astype(BF16)


def second_kernel(gaps, count, place_ref, delta, *refs):
    pieces, refs = refs[:count], refs[count:]
    before, out, gram, part, work = refs
    part[...] = before[...]
    peak = biggest(pieces)
    scale = power_scale(peak)
    second = power_scale(peak * (1.0 / LIFT), root=True)
    right_gram = None
    for piece in pieces:
        scaled = (piece[...].astype(F32) * scale).astype(BF16)
        term = dot(scaled, scaled, NT)
        right_gram = term if right_gram is None else right_gram + term
    inverse = inverse_factor(right_gram, work) * second
    add_products(place_ref[0], gaps, [pieces[gap] for gap in gaps], delta, part)
    left = dot_wide(inverse, part[...] * scale).astype(BF16)
    out[...] = left
    gram[...] = dot(left, left, NT)


def delta_call(kernel, place, delta, args, out_shape, scratch, name):
    vmem = pl.BlockSpec(memory_space=pltpu.VMEM)
    return pl.pallas_call(
        kernel,
        in_specs=[pl.BlockSpec(memory_space=pltpu.SMEM)] + [vmem] * (1 + len(args)),
        out_specs=[vmem] * len(out_shape),
        out_shape=out_shape,
        scratch_shapes=scratch,
        compiler_params=pltpu.CompilerParams(vmem_limit_bytes=DELTA_VMEM_BYTES),
        name=name,
        cost_estimate=SHORT,
    )(place, pltpu.with_memory_space_constraint(delta, pltpu.VMEM), *args)


def left_sweep(kernel, place, delta, own, early, out_shape, scratch, name):
    rank, width = own.shape
    rows = delta.shape[0]
    count = lax.axis_size("rows")
    near = tuple(gap for gap in range(1, count) if not gap & (gap - 1))
    far = tuple(gap for gap in range(1, count) if gap & (gap - 1))

    def add(gaps, args):
        return delta_call(
            functools.partial(part_kernel, gaps, gaps[0] == 0), place, delta, args,
            [jax.ShapeDtypeStruct((rank, rows), F32)], [], name + "_part",
        )[0]

    arrived = [permute(own, "rows", gap) for gap in near]
    if early:
        part = add((0,), [own])
        part, *arrived = together(part, *arrived)
    pieces = [own] + [None] * (count - 1)
    for gap, piece in zip(near, arrived):
        pieces[gap] = piece
    forward(pieces, "rows")
    part = add(near, [*arrived, part]) if early else add((0, *near), [own, *arrived])
    return delta_call(
        functools.partial(kernel, far, count), place, delta, [*pieces, part], out_shape,
        [pltpu.VMEM((rank, rows), F32)] + scratch, name,
    )


def right_kernel_first(gap, place_ref, delta, left, out):
    width = out.shape[1]
    step = 1792 if width % 1792 == 0 else width
    for start in range(0, width, step):
        at = pl.ds(pl.multiple_of((place_ref[0] ^ gap) * width + start, 128), step)
        out[:, start:start + step] = dot(left[...], delta[:, at]).astype(BF16)


def right_kernel_second(gap, real, place_ref, delta, left, out):
    groups, _, size = out.shape
    slot = place_ref[0] ^ gap
    start = slot_start(slot, size, real)
    inside = lax.broadcasted_iota(jnp.int32, (1, size), 1) + start >= slot * size
    for group in range(groups):
        at = pl.ds(pl.multiple_of(group * real + start, 128), size)
        value = dot(left[...], delta[:, at])
        out[group] = jnp.where(inside, value, 0.0).astype(BF16)


def own_kernel_second(count, real, place_ref, delta, left, *refs):
    grams, (out, unit, inverse, work) = refs[:count], refs[count:]
    right_kernel_second(0, real, place_ref, delta, left, out)
    total = grams[0][...]
    for gram in grams[1:]:
        total = total + gram[...]
    factor = inverse_factor(total, work)
    inverse[...] = factor
    high_part, low_part = halves(factor)
    unit[...] = (dot(high_part, left[...]) + dot(low_part, left[...])).astype(BF16)


def slot_start(slot, size, real):
    return jnp.minimum(slot * size, real - size)


def small_call(kernel, out_shape, args, scratch=(), name=None, scalars=0, hbm=0):
    spaces = [pltpu.SMEM] * scalars + [pltpu.HBM] * hbm + [pltpu.VMEM] * (len(args) - scalars - hbm)
    spec = lambda i: pl.BlockSpec(memory_space=spaces[i])
    return pl.pallas_call(
        kernel,
        in_specs=[spec(i) for i in range(len(args))],
        out_specs=[pl.BlockSpec(memory_space=pltpu.VMEM)] * len(out_shape),
        out_shape=out_shape,
        scratch_shapes=list(scratch),
        compiler_params=pltpu.CompilerParams(vmem_limit_bytes=VMEM_BYTES),
        name=name,
        cost_estimate=SHORT,
    )(*args)


def right_sum_kernel(count, *refs):
    parts, (total, gram) = refs[:count], refs[count:]
    result = None
    for group in range(total.shape[0]):
        value = parts[0][group].astype(F32)
        for part in parts[1:]:
            value = value + part[group].astype(F32)
        total[group] = value
        term = dot_wide(value, value, NT)
        result = term if result is None else result + term
    gram[...] = result


def right_kernel(count, groups, place_ref, weight_ref, total, left_inverse, *refs):
    grams, outs, (work,) = refs[:count], refs[count:count + groups], refs[count + groups:]
    gram = grams[0][...]
    for other in grams[1:]:
        gram = gram + other[...]
    factor = inverse_factor(gram, work)
    middle_high, middle_low = halves(weight_ref[0] * dot_wide(left_inverse[...], dot_wide(gram, factor, NT)))
    high, low = halves(factor)
    rank, size = total.shape[1:]
    for gap, out in enumerate(outs):
        value_high, value_low = halves(total[place_ref[0] ^ gap])
        out[:, :size] = (dot(high, value_high) + (dot(high, value_low) + dot(low, value_high))).astype(BF16)
        out[:, size:size + rank] = middle_high
        out[:, size + rank:] = middle_low


def grams_kernel(groups, place_ref, left_hbm, *refs):
    pieces, (stack, middles, home, away, left_rows, left_stack, sem) = refs[:groups], refs[groups:]
    copy = pltpu.make_async_copy(left_hbm, left_stack, sem)
    copy.start()
    rank = pieces[0].shape[0]
    size = stack.shape[1]
    place = place_ref[0]
    for gap, piece in enumerate(pieces):
        owner = place ^ gap
        stack[pl.ds(pl.multiple_of(owner * rank, rank), rank), :] = piece[:, :size]
        middles[owner] = piece[:, size:size + rank].astype(F32) + piece[:, size + rank:].astype(F32)
    for number in range(groups // 2):
        for out, gap in ((home, 2 * number), (away, 2 * number + 1)):
            at = pl.multiple_of((place ^ gap) * rank, rank)
            out[number] = dot(stack[pl.ds(at, rank), :], stack[...], NT).astype(BF16)
    copy.wait()
    at = pl.multiple_of(place * rank, rank)
    left_rows[...] = dot(left_stack[pl.ds(at, rank), :], left_stack[...], NT).astype(BF16)


def polish(count, sides):
    size = sides[0][0].shape[0]
    eye = (
        lax.broadcasted_iota(jnp.int32, (size, size), 0) == lax.broadcasted_iota(jnp.int32, (size, size), 1)
    ).astype(F32)
    lead, tail = 1.5 / math.sqrt(count), -0.5 / (count * math.sqrt(count))
    strip = min(512, size)
    for gram, product, _, _ in sides:
        product[...] = lead * eye + tail * gram[...]

    def multiply(a_ref, c_ref, other, lead, tail):
        def one(index, _):
            rows = pl.ds(pl.multiple_of(index * strip, strip), strip)
            a = a_ref[rows, :]
            c_ref[rows, :] = lead * a + tail * dot(a.astype(BF16), other[...])
            return 0

        if strip == size:
            c_ref[...] = lead * a_ref[...] + tail * dot(a_ref[...].astype(BF16), other[...])
        else:
            lax.fori_loop(0, size // strip, one, 0)

    def step(index, _):
        first = index == 1
        before = jnp.where(first, lead, 1.5)
        after = jnp.where(first, tail, -0.5)
        for gram, _, _, other in sides:
            other[...] = gram[...].astype(BF16)
        for gram, _, spare, other in sides:
            multiply(gram, spare, other, before, after)
        for gram, _, spare, other in sides:
            multiply(spare, gram, other, before, after)
        for gram, _, _, other in sides:
            other[...] = gram[...].astype(BF16)
        for _, product, _, other in sides:
            multiply(product, product, other, 1.5, -0.5)
        return 0

    lax.fori_loop(1, NS_ITERS, step, 0)


def merge_kernel(count, ckpt_count, places_ref, left_hbm, middle, *refs):
    columns, pieces, refs = refs[:2], refs[2], refs[3:]
    out, gram, product, spare, left_gram, left_product, left_spare, other, left_other, wide, strips, stack, sem, sems = refs
    real = out.shape[1]
    load = pltpu.make_async_copy(left_hbm, stack, sem)
    load.start()
    rank = middle.shape[1]
    for number in range(ckpt_count // 2):
        for side, column in enumerate(columns):
            rows = pl.ds(pl.multiple_of((places_ref[0] ^ (2 * number + side)) * rank, rank), rank)
            gram[rows, :] = column[number, :rank, :].astype(F32)
            left_gram[rows, :] = column[number, rank:, :].astype(F32)
    size = pieces.shape[2]
    wide[...] = jnp.zeros_like(wide)
    for slot in range(count):
        start = min(slot * size, real - size)
        wide[:, start:start + size] += pieces[slot]
    polish(ckpt_count, [(gram, product, spare, other), (left_gram, left_product, left_spare, left_other)])
    for index in range(ckpt_count):
        rows = pl.ds(index * rank, rank)
        left_spare[rows, :] = dot_wide(jnp.transpose(middle[index]), left_product[rows, :])
    other[...] = dot_wide(product[...], left_spare[...]).astype(BF16)

    load.wait()
    copies = []
    for number in range(strips.shape[0]):
        span = slice(number * strips.shape[1], (number + 1) * strips.shape[1])
        turned = jnp.transpose(dot(other[...], stack[:, span])).astype(BF16)
        strips[number] = dot(turned, wide[...]).astype(BF16)
        copy = pltpu.make_async_copy(strips.at[number], out.at[pl.ds(span.start, strips.shape[1]), :], sems.at[number])
        copy.start()
        copies.append(copy)
    for copy in copies:
        copy.wait()


def permute(value, axis, gap):
    count = lax.axis_size(axis)
    return lax.ppermute(value, axis, [(source, source ^ gap) for source in range(count)])


def spread(value, axis):
    return [value] + [permute(value, axis, gap) for gap in range(1, lax.axis_size(axis))]


def forward(got, axis):
    half = got[0].shape[0] // 2
    for gap in sorted(range(1, len(got)), key=lambda gap: bin(gap).count("1")):
        low, high = gap & -gap, 1 << (gap.bit_length() - 1)
        if low != high:
            got[gap] = jnp.concatenate([
                permute(got[gap ^ low][:half], axis, low), permute(got[gap ^ high][half:], axis, high)
            ])
    return got


def swap(values, axis):
    return [values[0]] + [permute(value, axis, gap) for gap, value in enumerate(values) if gap]


def right_sweep(call, left, count, small=()):
    parts = [None] * count
    for gap in range(count - 1, 0, -1):
        piece, left = together(call(gap, left), left)
        if small:
            left, *small = together(left, *small)
        parts[gap] = permute(piece, "rows", gap)
    if count > 2:
        left, parts[count - 1] = together(left, parts[count - 1])
    parts[0] = call(0, left, *small)
    return parts


def together(*values):
    return lax.optimization_barrier(values)


def add_up(values):
    return sum(value.astype(F32) for value in values)


def body(deltas, start_basis, edit_order):
    changes = deltas[0]
    start = jnp.transpose(start_basis[0])
    rank, width = start.shape
    rows, cols = changes.shape
    count = lax.axis_size("rows")
    groups = lax.axis_size("ckpt")
    row_place = lax.axis_index("rows").astype(jnp.int32)
    ckpt_place = lax.axis_index("ckpt").astype(jnp.int32)
    at_row = row_place[None]
    at_ckpt = ckpt_place[None]
    at_both = jnp.stack([ckpt_place, row_place])
    shape = jax.ShapeDtypeStruct
    square = shape((rank, rank), F32)
    work = pltpu.VMEM((rank, 2 * rank), F32)
    (left,) = left_sweep(
        first_kernel, at_row, changes, start, True, [shape((rank, rows), BF16)], [], "first_left"
    )
    parts = right_sweep(
        lambda gap, left: delta_call(
            functools.partial(right_kernel_first, gap), at_row, changes, [left], [shape((rank, width), BF16)], [],
            "first_right",
        )[0],
        left, count,
    )
    right = add_up(parts).astype(BF16)

    block = cols // groups
    padded = -(-block // (count * 128)) * 128
    left, left_gram = left_sweep(
        second_kernel, at_row, changes, right, True, [shape((rank, rows), BF16), square], [work], "second_left"
    )
    left_grams = spread(left_gram, "rows")

    def right_piece(gap, left, *grams):
        if gap:
            return delta_call(
                functools.partial(right_kernel_second, gap, block), at_row, changes, [left],
                [shape((groups, rank, padded), BF16)], [], "second_right",
            )[0]
        return delta_call(
            functools.partial(own_kernel_second, count, block), at_row, changes, [left, *grams],
            [shape((groups, rank, padded), BF16), shape((rank, rows), BF16), square], [work], "second_own",
        )

    parts = right_sweep(right_piece, left, count, left_grams)
    parts[0], left_unit, left_inverse = parts[0]
    left_unit, *arrived = together(left_unit, *parts[1:])
    parts[1:] = arrived
    left_stack = lax.all_gather(left_unit, "ckpt", axis=0, tiled=True)
    total, right_gram = small_call(
        functools.partial(right_sum_kernel, count), [shape((groups, rank, padded), F32), square], parts,
        name="right_sum",
    )
    position = jnp.sum(jnp.where(jnp.arange(groups) == ckpt_place, edit_order, 0))
    weight = (1 + position).astype(F32)[None] / groups
    leaving = small_call(
        functools.partial(right_kernel, count, groups), [shape((rank, padded + 2 * rank), BF16)] * groups,
        [at_ckpt, weight, total, left_inverse] + spread(right_gram, "rows"), [work], "right_unit", scalars=2,
    )
    pieces = swap(leaving, "ckpt")
    size = groups * rank
    slabs = shape((groups // 2, rank, size), BF16)
    in_hbm = pltpu.with_memory_space_constraint(left_stack, pltpu.HBM)
    right_stack, middles, home, away, left_rows = small_call(
        functools.partial(grams_kernel, groups),
        [shape((size, padded), BF16), shape((groups, rank, rank), F32), slabs, slabs, shape((rank, size), BF16)],
        [at_ckpt, in_hbm] + pieces, [pltpu.VMEM(left_stack.shape, BF16), pltpu.SemaphoreType.DMA(())],
        name="grams", scalars=1, hbm=1,
    )
    pair_sum = add_up([home, permute(away, "ckpt", 1)]).astype(BF16)
    gathered = lax.all_gather(right_stack, "rows", axis=0)
    own = add_up([pair_sum[0]] + [permute(pair_sum[n], "ckpt", 2 * n) for n in range(1, groups // 2)]).astype(BF16)
    both = add_up(spread(jnp.concatenate([own, left_rows]), "rows")).astype(BF16)
    column = jnp.stack([both] + [permute(both, "ckpt", gap) for gap in range(2, groups, 2)])
    columns = [column, permute(column, "ckpt", 1)]

    step = min(256, rows)
    vmem = pl.BlockSpec(memory_space=pltpu.VMEM)
    args = [in_hbm, middles, *columns, gathered]
    return pl.pallas_call(
        functools.partial(merge_kernel, count, groups),
        in_specs=[pl.BlockSpec(memory_space=pltpu.SMEM), pl.BlockSpec(memory_space=pltpu.HBM)] + [vmem] * (len(args) - 1),
        out_specs=pl.BlockSpec(memory_space=pl.ANY),
        out_shape=shape((rows, block), BF16),
        scratch_shapes=[pltpu.VMEM((size, size), F32)] * 6 + [pltpu.VMEM((size, size), BF16)] * 2
        + [pltpu.VMEM((size, block), BF16), pltpu.VMEM((rows // step, step, block), BF16),
           pltpu.VMEM(left_stack.shape, BF16), pltpu.SemaphoreType.DMA(()), pltpu.SemaphoreType.DMA((rows // step,))],
        compiler_params=pltpu.CompilerParams(vmem_limit_bytes=2 * VMEM_BYTES),
        name="merge",
        cost_estimate=SHORT,
    )(at_both, *args)


def solution(mesh):
    return jax.shard_map(
        body,
        mesh=mesh,
        in_specs=(P("ckpt", "rows", None), P("ckpt", "rows", None), P()),
        out_specs=P("rows", "ckpt"),
        check_vma=False,
    )
```

```python
import functools
import math

import jax
import jax.numpy as jnp
from jax import lax
from jax.experimental import pallas as pl
from jax.experimental.pallas import tpu as pltpu
from jax.sharding import PartitionSpec as P

NS_ITERS = 4
LIFT = 2.0**60
VMEM_BYTES = 24 * 1024 * 1024
DELTA_VMEM_BYTES = 22 * 1024 * 1024
SHORT = pl.CostEstimate(flops=1024, bytes_accessed=1024, transcendentals=0)
F32 = jnp.float32
BF16 = jnp.bfloat16
NN = (((1,), (0,)), ((), ()))
NT = (((1,), (1,)), ((), ()))
TN = (((0,), (0,)), ((), ()))


def dot(a, b, dims=NN):
    return lax.dot_general(a, b, dims, preferred_element_type=F32)


def halves(x):
    high = x.astype(BF16)
    return high, (x - high.astype(F32)).astype(BF16)


def dot_wide(a, b, dims=NN):
    a_high, a_low = halves(a)
    b_high, b_low = halves(b)
    return dot(a_high, b_high, dims) + (dot(a_high, b_low, dims) + dot(a_low, b_high, dims))


def power_scale(peak, root=False):
    scale = jnp.ones_like(peak)
    full = jnp.ones_like(peak)
    for exponent in (64, 32, 16, 8, 4, 2, 1):
        big = peak * full >= 2.0**exponent
        full = jnp.where(big, full * 2.0**-exponent, full)
        scale = jnp.where(big, scale * 2.0 ** -(exponent // 2), scale)
    for exponent in (64, 32, 16, 8, 4, 2, 1):
        small = peak * full * 2.0**exponent < 2.0
        full = jnp.where(small, full * 2.0**exponent, full)
        scale = jnp.where(small, scale * 2.0 ** (exponent // 2), scale)
    return scale if root else full


def inverse_factor(gram, work):
    rank = gram.shape[0]
    index = lax.broadcasted_iota(jnp.int32, (rank, 1), 0)
    lane = lax.broadcasted_iota(jnp.int32, (rank, 2 * rank), 1)
    work[:, :rank] = (lax.broadcasted_iota(jnp.int32, (rank, rank), 1) == index).astype(F32)
    work[:, rank:] = gram
    tiles = [work[at:at + 8, :] for at in range(0, rank, 8)]
    below = lax.broadcasted_iota(jnp.int32, (8, 2 * rank), 0)
    for k in range(rank - 1):
        at = rank + k
        first, inner = divmod(k, 8)
        columns = [jnp.broadcast_to(tile[:, at:at + 1], tile.shape) for tile in tiles[first:]]
        row = tiles[first][inner:inner + 1, :] * (1.0 / columns[0][inner:inner + 1, :])
        columns[0] = jnp.where(below > inner, columns[0], 0.0)
        for number, column in enumerate(columns, first):
            tiles[number] = tiles[number] - column * row
    table = jnp.concatenate(tiles, axis=0)
    pivots = jnp.sum(jnp.where(lane == index + rank, table, 0.0), axis=1, keepdims=True)
    work[...] = table * lax.rsqrt(pivots)
    return work[:, :rank]


def slot_columns(place, gap, width):
    return pl.ds(pl.multiple_of((place ^ gap) * width, 128), width)


def add_products(place, gaps, pieces, delta, part):
    rows = delta.shape[0]
    block = min(256, rows)
    for start in range(0, rows, block):
        total = part[:, start:start + block]
        for gap, piece in zip(gaps, pieces):
            columns = slot_columns(place, gap, piece.shape[1])
            total += dot(piece[...], delta[start:start + block, columns], NT)
        part[:, start:start + block] = total


def part_kernel(gaps, fresh, place_ref, delta, *refs):
    pieces, refs = refs[:len(gaps)], refs[len(gaps):]
    out = refs[-1]
    out[...] = jnp.zeros_like(out) if fresh else refs[0][...]
    add_products(place_ref[0], gaps, pieces, delta, out)


def biggest(pieces):
    peak = None
    for piece in pieces:
        most = jnp.max(jnp.abs(piece[...]).astype(F32), keepdims=True)
        peak = most if peak is None else jnp.maximum(peak, most)
    return peak


def first_kernel(gaps, count, place_ref, delta, *refs):
    pieces, refs = refs[:count], refs[count:]
    before, out, part = refs
    part[...] = before[...]
    scale = power_scale(biggest(pieces)) * LIFT
    add_products(place_ref[0], gaps, [pieces[gap] for gap in gaps], delta, part)
    out[...] = (part[...] * scale).astype(BF16)


def second_kernel(gaps, count, place_ref, delta, *refs):
    pieces, refs = refs[:count], refs[count:]
    before, out, gram, part, work = refs
    part[...] = before[...]
    peak = biggest(pieces)
    scale = power_scale(peak)
    second = power_scale(peak * (1.0 / LIFT), root=True)
    right_gram = None
    for piece in pieces:
        scaled = (piece[...].astype(F32) * scale).astype(BF16)
        term = dot(scaled, scaled, NT)
        right_gram = term if right_gram is None else right_gram + term
    inverse = inverse_factor(right_gram, work) * second
    add_products(place_ref[0], gaps, [pieces[gap] for gap in gaps], delta, part)
    left = dot_wide(inverse, part[...] * scale).astype(BF16)
    out[...] = left
    gram[...] = dot(left, left, NT)


def delta_call(kernel, place, delta, args, out_shape, scratch, name):
    vmem = pl.BlockSpec(memory_space=pltpu.VMEM)
    return pl.pallas_call(
        kernel,
        in_specs=[pl.BlockSpec(memory_space=pltpu.SMEM)] + [vmem] * (1 + len(args)),
        out_specs=[vmem] * len(out_shape),
        out_shape=out_shape,
        scratch_shapes=scratch,
        compiler_params=pltpu.CompilerParams(vmem_limit_bytes=DELTA_VMEM_BYTES),
        name=name,
        cost_estimate=SHORT,
    )(place, pltpu.with_memory_space_constraint(delta, pltpu.VMEM), *args)


def left_sweep(kernel, place, delta, own, early, out_shape, scratch, name):
    rank, width = own.shape
    rows = delta.shape[0]
    count = lax.axis_size("rows")
    near = tuple(gap for gap in range(1, count) if not gap & (gap - 1))
    far = tuple(gap for gap in range(1, count) if gap & (gap - 1))

    def add(gaps, args):
        return delta_call(
            functools.partial(part_kernel, gaps, gaps[0] == 0), place, delta, args,
            [jax.ShapeDtypeStruct((rank, rows), F32)], [], name + "_part",
        )[0]

    arrived = [permute(own, "rows", gap) for gap in near]
    if early:
        part = add((0,), [own])
        part, *arrived = together(part, *arrived)
    pieces = [own] + [None] * (count - 1)
    for gap, piece in zip(near, arrived):
        pieces[gap] = piece
    forward(pieces, "rows")
    part = add(near, [*arrived, part]) if early else add((0, *near), [own, *arrived])
    return delta_call(
        functools.partial(kernel, far, count), place, delta, [*pieces, part], out_shape,
        [pltpu.VMEM((rank, rows), F32)] + scratch, name,
    )


def right_kernel_first(gap, place_ref, delta, left, out):
    width = out.shape[1]
    step = 1792 if width % 1792 == 0 else width
    for start in range(0, width, step):
        at = pl.ds(pl.multiple_of((place_ref[0] ^ gap) * width + start, 128), step)
        out[:, start:start + step] = dot(left[...], delta[:, at]).astype(BF16)


def right_kernel_second(gap, real, place_ref, delta, left, out):
    groups, _, size = out.shape
    slot = place_ref[0] ^ gap
    start = slot_start(slot, size, real)
    inside = lax.broadcasted_iota(jnp.int32, (1, size), 1) + start >= slot * size
    for group in range(groups):
        at = pl.ds(pl.multiple_of(group * real + start, 128), size)
        value = dot(left[...], delta[:, at])
        out[group] = jnp.where(inside, value, 0.0).astype(BF16)


def own_kernel_second(count, real, place_ref, delta, left, *refs):
    grams, (out, unit, inverse, work) = refs[:count], refs[count:]
    right_kernel_second(0, real, place_ref, delta, left, out)
    total = grams[0][...]
    for gram in grams[1:]:
        total = total + gram[...]
    factor = inverse_factor(total, work)
    inverse[...] = factor
    high_part, low_part = halves(factor)
    unit[...] = (dot(high_part, left[...]) + dot(low_part, left[...])).astype(BF16)


def slot_start(slot, size, real):
    return jnp.minimum(slot * size, real - size)


def small_call(kernel, out_shape, args, scratch=(), name=None, scalars=0, hbm=0):
    spaces = [pltpu.SMEM] * scalars + [pltpu.HBM] * hbm + [pltpu.VMEM] * (len(args) - scalars - hbm)
    spec = lambda i: pl.BlockSpec(memory_space=spaces[i])
    return pl.pallas_call(
        kernel,
        in_specs=[spec(i) for i in range(len(args))],
        out_specs=[pl.BlockSpec(memory_space=pltpu.VMEM)] * len(out_shape),
        out_shape=out_shape,
        scratch_shapes=list(scratch),
        compiler_params=pltpu.CompilerParams(vmem_limit_bytes=VMEM_BYTES),
        name=name,
        cost_estimate=SHORT,
    )(*args)


def right_sum_kernel(count, *refs):
    parts, (total, gram) = refs[:count], refs[count:]
    result = None
    for group in range(total.shape[0]):
        value = parts[0][group].astype(F32)
        for part in parts[1:]:
            value = value + part[group].astype(F32)
        total[group] = value
        term = dot_wide(value, value, NT)
        result = term if result is None else result + term
    gram[...] = result


def right_kernel(count, groups, place_ref, weight_ref, total, left_inverse, *refs):
    grams, outs, (work,) = refs[:count], refs[count:count + groups], refs[count + groups:]
    gram = grams[0][...]
    for other in grams[1:]:
        gram = gram + other[...]
    factor = inverse_factor(gram, work)
    middle_high, middle_low = halves(weight_ref[0] * dot_wide(left_inverse[...], dot_wide(gram, factor, NT)))
    high, low = halves(factor)
    rank, size = total.shape[1:]
    for gap, out in enumerate(outs):
        value_high, value_low = halves(total[place_ref[0] ^ gap])
        out[:, :size] = (dot(high, value_high) + (dot(high, value_low) + dot(low, value_high))).astype(BF16)
        out[:, size:size + rank] = middle_high
        out[:, size + rank:] = middle_low


def grams_kernel(groups, place_ref, left_hbm, *refs):
    pieces, (stack, middles, home, away, left_rows, left_stack, sem) = refs[:groups], refs[groups:]
    copy = pltpu.make_async_copy(left_hbm, left_stack, sem)
    copy.start()
    rank = pieces[0].shape[0]
    size = stack.shape[1]
    place = place_ref[0]
    for gap, piece in enumerate(pieces):
        owner = place ^ gap
        stack[pl.ds(pl.multiple_of(owner * rank, rank), rank), :] = piece[:, :size]
        middles[owner] = piece[:, size:size + rank].astype(F32) + piece[:, size + rank:].astype(F32)
    for number in range(groups // 2):
        for out, gap in ((home, 2 * number), (away, 2 * number + 1)):
            at = pl.multiple_of((place ^ gap) * rank, rank)
            out[number] = dot(stack[pl.ds(at, rank), :], stack[...], NT).astype(BF16)
    copy.wait()
    at = pl.multiple_of(place * rank, rank)
    left_rows[...] = dot(left_stack[pl.ds(at, rank), :], left_stack[...], NT).astype(BF16)


def polish(count, sides):
    size = sides[0][0].shape[0]
    eye = (
        lax.broadcasted_iota(jnp.int32, (size, size), 0) == lax.broadcasted_iota(jnp.int32, (size, size), 1)
    ).astype(F32)
    lead, tail = 1.5 / math.sqrt(count), -0.5 / (count * math.sqrt(count))
    strip = min(512, size)
    for gram, product, _, _ in sides:
        product[...] = lead * eye + tail * gram[...]

    def multiply(a_ref, c_ref, other, lead, tail):
        def one(index, _):
            rows = pl.ds(pl.multiple_of(index * strip, strip), strip)
            a = a_ref[rows, :]
            c_ref[rows, :] = lead * a + tail * dot(a.astype(BF16), other[...])
            return 0

        if strip == size:
            c_ref[...] = lead * a_ref[...] + tail * dot(a_ref[...].astype(BF16), other[...])
        else:
            lax.fori_loop(0, size // strip, one, 0)

    def step(index, _):
        first = index == 1
        before = jnp.where(first, lead, 1.5)
        after = jnp.where(first, tail, -0.5)
        for gram, _, _, other in sides:
            other[...] = gram[...].astype(BF16)
        for gram, _, spare, other in sides:
            multiply(gram, spare, other, before, after)
        for gram, _, spare, other in sides:
            multiply(spare, gram, other, before, after)
        for gram, _, _, other in sides:
            other[...] = gram[...].astype(BF16)
        for _, product, _, other in sides:
            multiply(product, product, other, 1.5, -0.5)
        return 0

    lax.fori_loop(1, NS_ITERS, step, 0)


def merge_kernel(count, ckpt_count, places_ref, left_hbm, right_hbm, middle, *refs):
    columns, refs = refs[:2], refs[2:]
    out, gram, product, spare, left_gram, left_product, left_spare, other, left_other, wide, strips, stack, sem, sems, pieces, right_sem = refs
    real = out.shape[1]
    load = pltpu.make_async_copy(left_hbm, stack, sem)
    load.start()
    right_load = pltpu.make_async_copy(right_hbm, pieces, right_sem)
    right_load.start()
    rank = middle.shape[1]
    for number in range(ckpt_count // 2):
        for side, column in enumerate(columns):
            rows = pl.ds(pl.multiple_of((places_ref[0] ^ (2 * number + side)) * rank, rank), rank)
            gram[rows, :] = column[number, :rank, :].astype(F32)
            left_gram[rows, :] = column[number, rank:, :].astype(F32)
    polish(ckpt_count, [(gram, product, spare, other), (left_gram, left_product, left_spare, left_other)])
    for index in range(ckpt_count):
        rows = pl.ds(index * rank, rank)
        left_spare[rows, :] = dot_wide(jnp.transpose(middle[index]), left_product[rows, :])
    other[...] = dot_wide(product[...], left_spare[...]).astype(BF16)

    right_load.wait()
    size = pieces.shape[2]
    wide[...] = jnp.zeros_like(wide)
    for slot in range(count):
        start = min(slot * size, real - size)
        wide[:, start:start + size] += pieces[slot]
    load.wait()
    copies = []
    for number in range(strips.shape[0]):
        span = slice(number * strips.shape[1], (number + 1) * strips.shape[1])
        turned = jnp.transpose(dot(other[...], stack[:, span])).astype(BF16)
        strips[number] = dot(turned, wide[...]).astype(BF16)
        copy = pltpu.make_async_copy(strips.at[number], out.at[pl.ds(span.start, strips.shape[1]), :], sems.at[number])
        copy.start()
        copies.append(copy)
    for copy in copies:
        copy.wait()


def permute(value, axis, gap):
    count = lax.axis_size(axis)
    return lax.ppermute(value, axis, [(source, source ^ gap) for source in range(count)])


def spread(value, axis):
    return [value] + [permute(value, axis, gap) for gap in range(1, lax.axis_size(axis))]


def forward(got, axis):
    half = got[0].shape[0] // 2
    for gap in sorted(range(1, len(got)), key=lambda gap: bin(gap).count("1")):
        low, high = gap & -gap, 1 << (gap.bit_length() - 1)
        if low != high:
            got[gap] = jnp.concatenate([
                permute(got[gap ^ low][:half], axis, low), permute(got[gap ^ high][half:], axis, high)
            ])
    return got


def swap(values, axis):
    return [values[0]] + [permute(value, axis, gap) for gap, value in enumerate(values) if gap]


def right_sweep(call, left, count, small=()):
    parts = [None] * count
    for gap in range(count - 1, 0, -1):
        piece, left = together(call(gap, left), left)
        if small:
            left, *small = together(left, *small)
        parts[gap] = permute(piece, "rows", gap)
    if count > 2:
        left, parts[count - 1] = together(left, parts[count - 1])
    parts[0] = call(0, left, *small)
    return parts


def together(*values):
    return lax.optimization_barrier(values)


def add_up(values):
    return sum(value.astype(F32) for value in values)


def body(deltas, start_basis, edit_order):
    changes = deltas[0]
    start = jnp.transpose(start_basis[0])
    rank, width = start.shape
    rows, cols = changes.shape
    count = lax.axis_size("rows")
    groups = lax.axis_size("ckpt")
    row_place = lax.axis_index("rows").astype(jnp.int32)
    ckpt_place = lax.axis_index("ckpt").astype(jnp.int32)
    at_row = row_place[None]
    at_ckpt = ckpt_place[None]
    at_both = jnp.stack([ckpt_place, row_place])
    shape = jax.ShapeDtypeStruct
    square = shape((rank, rank), F32)
    work = pltpu.VMEM((rank, 2 * rank), F32)
    (left,) = left_sweep(
        first_kernel, at_row, changes, start, True, [shape((rank, rows), BF16)], [], "first_left"
    )
    parts = right_sweep(
        lambda gap, left: delta_call(
            functools.partial(right_kernel_first, gap), at_row, changes, [left], [shape((rank, width), BF16)], [],
            "first_right",
        )[0],
        left, count,
    )
    right = add_up(parts).astype(BF16)

    block = cols // groups
    padded = -(-block // (count * 128)) * 128
    left, left_gram = left_sweep(
        second_kernel, at_row, changes, right, True, [shape((rank, rows), BF16), square], [work], "second_left"
    )
    left_grams = spread(left_gram, "rows")

    def right_piece(gap, left, *grams):
        if gap:
            return delta_call(
                functools.partial(right_kernel_second, gap, block), at_row, changes, [left],
                [shape((groups, rank, padded), BF16)], [], "second_right",
            )[0]
        return delta_call(
            functools.partial(own_kernel_second, count, block), at_row, changes, [left, *grams],
            [shape((groups, rank, padded), BF16), shape((rank, rows), BF16), square], [work], "second_own",
        )

    parts = right_sweep(right_piece, left, count, left_grams)
    parts[0], left_unit, left_inverse = parts[0]
    left_unit, *arrived = together(left_unit, *parts[1:])
    parts[1:] = arrived
    left_stack = lax.all_gather(left_unit, "ckpt", axis=0, tiled=True)
    total, right_gram = small_call(
        functools.partial(right_sum_kernel, count), [shape((groups, rank, padded), F32), square], parts,
        name="right_sum",
    )
    position = jnp.sum(jnp.where(jnp.arange(groups) == ckpt_place, edit_order, 0))
    weight = (1 + position).astype(F32)[None] / groups
    leaving = small_call(
        functools.partial(right_kernel, count, groups), [shape((rank, padded + 2 * rank), BF16)] * groups,
        [at_ckpt, weight, total, left_inverse] + spread(right_gram, "rows"), [work], "right_unit", scalars=2,
    )
    pieces = swap(leaving, "ckpt")
    size = groups * rank
    slabs = shape((groups // 2, rank, size), BF16)
    in_hbm = pltpu.with_memory_space_constraint(left_stack, pltpu.HBM)
    right_stack, middles, home, away, left_rows = small_call(
        functools.partial(grams_kernel, groups),
        [shape((size, padded), BF16), shape((groups, rank, rank), F32), slabs, slabs, shape((rank, size), BF16)],
        [at_ckpt, in_hbm] + pieces, [pltpu.VMEM(left_stack.shape, BF16), pltpu.SemaphoreType.DMA(())],
        name="grams", scalars=1, hbm=1,
    )
    pair_sum = add_up([home, permute(away, "ckpt", 1)]).astype(BF16)
    gathered = lax.all_gather(right_stack, "rows", axis=0)
    own = add_up([pair_sum[0]] + [permute(pair_sum[n], "ckpt", 2 * n) for n in range(1, groups // 2)]).astype(BF16)
    both = add_up(spread(jnp.concatenate([own, left_rows]), "rows")).astype(BF16)
    column = jnp.stack([both] + [permute(both, "ckpt", gap) for gap in range(2, groups, 2)])
    columns = [column, permute(column, "ckpt", 1)]

    step = min(256, rows)
    vmem = pl.BlockSpec(memory_space=pltpu.VMEM)
    args = [in_hbm, pltpu.with_memory_space_constraint(gathered, pltpu.HBM), middles, *columns]
    return pl.pallas_call(
        functools.partial(merge_kernel, count, groups),
        in_specs=[pl.BlockSpec(memory_space=pltpu.SMEM)] + [pl.BlockSpec(memory_space=pltpu.HBM)] * 2
        + [vmem] * (len(args) - 2),
        out_specs=pl.BlockSpec(memory_space=pl.ANY),
        out_shape=shape((rows, block), BF16),
        scratch_shapes=[pltpu.VMEM((size, size), F32)] * 6 + [pltpu.VMEM((size, size), BF16)] * 2
        + [pltpu.VMEM((size, block), BF16), pltpu.VMEM((rows // step, step, block), BF16),
           pltpu.VMEM(left_stack.shape, BF16), pltpu.SemaphoreType.DMA(()), pltpu.SemaphoreType.DMA((rows // step,)),
           pltpu.VMEM(gathered.shape, BF16), pltpu.SemaphoreType.DMA(())],
        compiler_params=pltpu.CompilerParams(vmem_limit_bytes=2 * VMEM_BYTES),
        name="merge",
        cost_estimate=SHORT,
    )(at_both, *args)


def solution(mesh):
    return jax.shard_map(
        body,
        mesh=mesh,
        in_specs=(P("ckpt", "rows", None), P("ckpt", "rows", None), P()),
        out_specs=P("rows", "ckpt"),
        check_vma=False,
    )
```
